32 devices in a mesh: pts: 16 (over z, y, core), cam: 2 (over x).
Axes of the slice: x: 2, y: 2, z: 4, core: 2. Of those that a mesh axis runs over, the one named last changes fastest.
Arguments:
- rhs: float32 [2, 128, 576], P('cam', 'pts'), may hold values from -6 to 6
- damp_cam: float32 [2, 128, 576], P('cam', 'pts'), may hold values from 0.2 to 1
- precond: float32 [2, 128, 576], P('cam', 'pts'), may hold values from 0.3 to 3
- cam_jac: float32 [2, 1536, 8, 18, 128], P('cam', 'pts'), may hold values from -0.3125 to 0.3125
- pt_jac: float32 [2, 1536, 8, 6, 128], P('cam', 'pts'), may hold values from -6 to 6
- damp_pt: float32 [2, 1536, 3, 128], P('cam', 'pts'), may hold values from 0.5 to 8
- cam_index: int32 [2, 1536, 8, 128], P('cam', 'pts'), may hold values from 0 to 63
- tile_ids: int32 [2, 1536, 8], P('cam', 'pts'), may hold values from 0 to 255, as said below
- counts: int32 [2, 1536], P('cam', 'pts'), may hold values from 2 to 8, as said below
Outputs:
- solution: float32 [2, 128, 576], P('cam', 'pts')
- residual: float32 [2, 128, 576], P('cam', 'pts')
The draws below stay inside these ranges and needn't reach their ends.
Inputs may be any that keep to these rules, and one draw needn't show every extreme that they name: `tile_ids`: point tile t of a group (t from 0 to 1535) lists only window tiles from (t * 128) // 1536 to that plus 128; entries at or beyond the tile's count are padding within the same range. `counts`: in every group the first point tile has all 8 entries live.
All inputs are finite; a program needn't handle non-finite values.
Results may differ from the reference program's by a relative error of at most 0.0003.
Values sent between devices are 32-bit elements; how exact they have to be, the bound alone decides.
No kernel may reach another device: no remote copies, remote signals or barrier semaphores. Data moves between devices by JAX's collectives and lax.ppermute only.
A program may use at most 64 MiB of HBM per device.

```python
import math
import jax
import jax.numpy as jnp
from jax import lax

CAMS = 64
CPAR = 9
PP = 128
SLOTS = 8
ITERS = 3
CT_DEV = 8
PT_DEV = 96
TILE = 576
GROUPS = 2
CT_GROUP = 128
PT_GROUP = 1536
HALF = 64


def draw_tile_ids(key, part):
    position = jnp.arange(PT_GROUP, dtype=jnp.int32)
    start = position * CT_GROUP // PT_GROUP
    offsets = jax.random.randint(key, (GROUPS, PT_GROUP, SLOTS), 0, CT_GROUP + 1)
    offsets = offsets.at[:, 0, 0].set(0)
    offsets = offsets.at[:, PT_GROUP - 1, 0].set(CT_GROUP)
    return (start[None, :, None] + offsets).astype(jnp.int32)


def draw_counts(key, part):
    counts = jax.random.randint(key, (GROUPS, PT_GROUP), 2, SLOTS + 1)
    counts = counts.at[:, 0].set(SLOTS)
    counts = counts.at[:, 1].set(2)
    return counts.astype(jnp.int32)


def touch_ends(drawn, own_key, least, largest):
    dims = drawn.shape
    spot = [jax.random.randint(jax.random.fold_in(own_key, axis), (), 0, dims[axis]) for axis in range(len(dims))]
    drawn = drawn.at[tuple(spot)].set(least)
    longest = dims.index(max(dims))
    spot[longest] = (spot[longest] + 1) % dims[longest]
    return drawn.at[tuple(spot)].set(largest)


def levels(rng, shape, cuts, smallest, high):
    factor_of, own = 1.0, jax.random.fold_in(rng, 6)
    for dim, shards_of in cuts:
        steps = jnp.exp(jax.random.uniform(jax.random.fold_in(own, dim), (shards_of,), jnp.float32, smallest / len(cuts), high / len(cuts)))
        factor_of = factor_of * jnp.repeat(steps, shape[dim] // shards_of).reshape([-1 if axis == dim else 1 for axis in range(len(shape))])
    return factor_of


def bell_draw(own_key, extent, width, bound, split=(), kind=jnp.bfloat16):
    result = width * jax.random.normal(own_key, extent, jnp.float32)
    if split:
        result = result * levels(own_key, extent, split, -0.22, 0.18)
    return jnp.clip(result, -bound, bound).astype(kind)


def setup_inputs(seed: int = 0) -> dict:
    key_of = jax.random.split(jax.random.key(seed), 10)
    rhs = bell_draw(key_of[0], (GROUPS, CT_GROUP, TILE), 1.0, 6.0, ((0, 2), (1, 16)), jnp.float32)
    damp_cam = jnp.clip(jnp.exp(math.log(1.0) - 1.609438 * jax.random.uniform(key_of[1], (GROUPS, CT_GROUP, TILE), jnp.float32) ** levels(key_of[1], (GROUPS, CT_GROUP, TILE), ((0, 2), (1, 16)), -0.2, 0.2)), 0.2, 1.0)
    precond = jnp.clip(jnp.exp(math.log(3.0) - 2.3025851 * jax.random.uniform(key_of[2], (GROUPS, CT_GROUP, TILE), jnp.float32) ** levels(key_of[2], (GROUPS, CT_GROUP, TILE), ((0, 2), (1, 16)), -0.2, 0.2)), 0.3, 3.0)
    cam_jac = bell_draw(key_of[3], (GROUPS, PT_GROUP, SLOTS, 2 * CPAR, PP), (2 * PT_DEV * PP * SLOTS // (CT_DEV * CAMS)) ** -0.5, 0.3125, ((0, 2), (1, 16)), jnp.float32)
    pt_jac = bell_draw(key_of[4], (GROUPS, PT_GROUP, SLOTS, 6, PP), 1.0, 6.0, ((0, 2), (1, 16)), jnp.float32)
    damp_pt = jnp.clip(jnp.exp(math.log(8.0) - 2.7725887 * jax.random.uniform(key_of[5], (GROUPS, PT_GROUP, 3, PP), jnp.float32) ** levels(key_of[5], (GROUPS, PT_GROUP, 3, PP), ((0, 2), (1, 16)), -0.2, 0.2)), 0.5, 8.0)
    cam_index = touch_ends(jax.random.randint(key_of[6], (GROUPS, PT_GROUP, SLOTS, PP), 0, CAMS), jax.random.fold_in(key_of[6], 1), 0, CAMS - 1).astype(jnp.int32)
    tile_ids = draw_tile_ids(jax.random.fold_in(key_of[9], 71), 0)
    counts = draw_counts(jax.random.fold_in(key_of[9], 71), 0)
    return dict(rhs=rhs, damp_cam=damp_cam, precond=precond, cam_jac=cam_jac, pt_jac=pt_jac, damp_pt=damp_pt, cam_index=cam_index, tile_ids=tile_ids, counts=counts)


def point_inverse(pt_jac, counts, damp_pt):
    tiles = pt_jac.shape[0]
    points = pt_jac.shape[-1]
    live = (jnp.arange(SLOTS, dtype=jnp.int32)[None, :] < counts[:, None]).astype(jnp.float32)
    shaped = pt_jac.reshape(tiles, SLOTS, 2, 3, points)
    gram = jnp.sum(live[:, :, None, None, None, None] * shaped[:, :, :, :, None, :] * shaped[:, :, :, None, :, :], axis=(1, 2))
    gram = gram + damp_pt[:, :, None, :] * jnp.eye(3, dtype=jnp.float32)[None, :, :, None]
    first = jnp.roll(jnp.roll(gram, -1, axis=1), -1, axis=2)
    second = jnp.roll(jnp.roll(gram, -2, axis=1), -2, axis=2)
    mixed_one = jnp.roll(jnp.roll(gram, -1, axis=1), -2, axis=2)
    mixed_two = jnp.roll(jnp.roll(gram, -2, axis=1), -1, axis=2)
    cofactor = first * second - mixed_one * mixed_two
    determinant = jnp.sum(gram[:, 0] * cofactor[:, 0], axis=1)
    return cofactor / determinant[:, None, None, :]


def group_term(items):
    window, cam_jac, pt_jac, cam_index, tile_ids, live, inverse = items
    grid = window.reshape(2 * CT_GROUP, CPAR, CAMS)
    params = jnp.arange(CPAR, dtype=jnp.int32)
    picked = grid[tile_ids[:, :, None, None], params[None, None, :, None], cam_index[:, :, None, :]]
    cam_rows = cam_jac.reshape(PT_GROUP, SLOTS, 2, CPAR, PP)
    point_rows = pt_jac.reshape(PT_GROUP, SLOTS, 2, 3, PP)
    masked = live[:, :, None, None]
    residual_rows = jnp.sum(cam_rows * picked[:, :, None], axis=3) * masked
    point_side = jnp.sum(point_rows * residual_rows[:, :, :, None, :], axis=(1, 2))
    solved = jnp.sum(inverse * point_side[:, None, :, :], axis=2)
    errors = (residual_rows - jnp.sum(point_rows * solved[:, None, None, :, :], axis=3)) * masked
    returned = jnp.sum(cam_rows * errors[:, :, :, None, :], axis=2)
    flat_ids = (tile_ids[:, :, None] * CAMS + cam_index).reshape(-1)
    values = jnp.transpose(returned, (0, 1, 3, 2)).reshape(-1, CPAR)
    summed = jax.ops.segment_sum(values, flat_ids, num_segments=2 * CT_GROUP * CAMS)
    return jnp.transpose(summed.reshape(2 * CT_GROUP, CAMS, CPAR), (0, 2, 1)).reshape(2 * CT_GROUP, TILE)


def reference(rhs, damp_cam, precond, cam_jac, pt_jac, damp_pt, cam_index, tile_ids, counts):
    live = (jnp.arange(SLOTS, dtype=jnp.int32)[None, None, :] < counts[:, :, None]).astype(jnp.float32)
    inverse = lax.map(lambda items: point_inverse(items[0], items[1], items[2]), (pt_jac, counts, damp_pt))

    def product(vector):
        lower = jnp.roll(vector, 1, axis=0)[:, HALF:]
        upper = jnp.roll(vector, -1, axis=0)[:, :HALF]
        windows = jnp.concatenate([lower, vector, upper], axis=1)
        partial_value = lax.map(group_term, (windows, cam_jac, pt_jac, cam_index, tile_ids, live, inverse))
        middle = partial_value[:, HALF:HALF + CT_GROUP]
        from_below = jnp.roll(partial_value[:, HALF + CT_GROUP:], 1, axis=0)
        from_above = jnp.roll(partial_value[:, :HALF], -1, axis=0)
        return middle + jnp.concatenate([from_below, from_above], axis=1) + damp_cam * vector

    solution = jnp.zeros(rhs.shape, jnp.float32)
    residual = rhs
    scaled = precond * residual
    direction = scaled
    energy = jnp.sum(residual * scaled)
    for iteration in range(ITERS):
        mapped = product(direction)
        step_size = energy / jnp.sum(direction * mapped)
        solution = solution + step_size * direction
        residual = residual - step_size * mapped
        scaled = precond * residual
        energy_next = jnp.sum(residual * scaled)
        direction = scaled + (energy_next / energy) * direction
        energy = energy_next
    return solution, residual
```

```python
import functools

import jax
import jax.numpy as jnp
from jax import lax
from jax.experimental import pallas as pl
from jax.experimental.pallas import tpu as pltpu
from jax.sharding import PartitionSpec as P

ITERS = 3
CPAR = 9
CAMERAS = 64
SLOTS = 8
POINTS = 128
TILE = CPAR * CAMERAS
PAIRS = 5
WIDTH = PAIRS * 128
BLOCK = 16
AXES = ("pts", "cam")
VMEM = pltpu.MemorySpace.VMEM


def split_two(value):
    high = value.astype(jnp.bfloat16)
    low = (value - high.astype(jnp.float32)).astype(jnp.bfloat16)
    return high, low


def over_slots(value):
    return jnp.sum(value, axis=0, keepdims=True)


def invert(gram):
    a, b, c, d, e, f = gram
    aa = d * f - e * e
    bb = c * e - b * f
    cc = b * e - c * d
    dd = a * f - c * c
    ee = b * c - a * e
    ff = a * d - b * b
    scale = 1.0 / (a * aa + b * bb + c * cc)
    return [entry * scale for entry in (aa, bb, cc, dd, ee, ff)]


def tile_product(count, cam, point, index, picked_from, row, inverse, damp, put_to):
    slot = lax.broadcasted_iota(jnp.int32, (SLOTS, POINTS), 0)
    lane = lax.broadcasted_iota(jnp.int32, (SLOTS, POINTS), 1)
    live = (slot < count).astype(jnp.float32)
    other = index + CAMERAS
    pairs = [picked_from[pl.ds(row, SLOTS), p * 128 : (p + 1) * 128] for p in range(PAIRS)]
    picked = [
        jnp.take_along_axis(
            pairs[j // 2], other if j % 2 else index, axis=1, mode="promise_in_bounds"
        )
        for j in range(CPAR)
    ]
    rows = [point(r) * live for r in range(6)]
    if inverse is None:
        entries = [(0, 0), (0, 1), (0, 2), (1, 1), (1, 2), (2, 2)]
        gram = [over_slots(rows[i] * rows[j] + rows[3 + i] * rows[3 + j]) for i, j in entries]
        for a, place in enumerate((0, 3, 5)):
            gram[place] = gram[place] + damp[a]
        inverse = invert(gram)
    q = []
    for r in range(2):
        total = cam(9 * r) * picked[0]
        for j in range(1, CPAR):
            total = total + cam(9 * r + j) * picked[j]
        q.append(total * live)
    y = [over_slots(rows[a] * q[0] + rows[3 + a] * q[1]) for a in range(3)]
    i0, i1, i2, i3, i4, i5 = inverse
    z = [
        i0 * y[0] + i1 * y[1] + i2 * y[2],
        i1 * y[0] + i3 * y[1] + i4 * y[2],
        i2 * y[0] + i4 * y[1] + i5 * y[2],
    ]
    e = [
        (q[r] - (rows[3 * r] * z[0] + rows[3 * r + 1] * z[1] + rows[3 * r + 2] * z[2])) * live
        for r in range(2)
    ]
    slot_twice = lax.broadcasted_iota(jnp.int32, (2 * SLOTS, POINTS), 0) & 1
    odd = slot_twice.astype(jnp.bfloat16)
    even = (1 - slot_twice).astype(jnp.bfloat16)
    left = []
    for j in range(CPAR):
        returned = cam(j) * e[0] + cam(9 + j) * e[1]
        high = returned.astype(jnp.bfloat16).astype(jnp.float32)
        both = jnp.concatenate([high, returned - high], axis=0).astype(jnp.bfloat16)
        left.append(jnp.concatenate([both * even, both * odd], axis=1))
    left = jnp.concatenate(left, axis=0)
    camera = lax.broadcasted_iota(jnp.int32, (CAMERAS, POINTS), 0)
    selector = []
    for pair in range(SLOTS // 2):
        halves = [
            (camera == index[k : k + 1, :]).astype(jnp.float32).astype(jnp.bfloat16)
            for k in (2 * pair, 2 * pair + 1)
        ]
        selector.append(jnp.concatenate(halves, axis=1))
    selector = jnp.concatenate(selector, axis=0)
    spread = lax.dot_general(
        left, selector, (((1,), (1,)), ((), ())), preferred_element_type=jnp.float32
    )
    side = (slot >> 1) & 1
    first_side = side == 0
    keep = (lane >> 6) == side
    sums = []
    for j in range(CPAR):
        both = spread[16 * j : 16 * j + 8] + spread[16 * j + 8 : 16 * j + 16]
        sums.append(jnp.where(slot < 4, both[:, :128], both[:, 128:]))
    sums.append(jnp.zeros_like(sums[0]))
    for p in range(PAIRS):
        one, two = sums[2 * p], sums[2 * p + 1]
        stay = jnp.where(first_side, one, two)
        move = pltpu.roll(jnp.where(first_side, two, one), CAMERAS, 1)
        put_to[pl.ds(row, SLOTS), p * 128 : (p + 1) * 128] = jnp.where(keep, stay, move)
    return q[0] * e[0] + q[1] * e[1], inverse


def product_steps(counts, cam, point, index, extra, pick, put, vector, out, inverse_out, dot, picked_from, put_to, before, after):
    step = pl.program_id(0)
    block = cam.shape[0]
    first = inverse_out is not None

    @pl.when(step == 0)
    def _():
        before()
        high, low = split_two(vector[...])
        picked_from[...] = jnp.dot(
            pick[...], high, preferred_element_type=jnp.float32
        ) + jnp.dot(pick[...], low, preferred_element_type=jnp.float32)
        dot[...] = jnp.zeros_like(dot)

    def advance(i, total):
        tile = step * block + i
        rows = [extra[a, pl.ds(i, 1), :] for a in range(extra.shape[0])]
        term, inverse = tile_product(
            counts[tile],
            lambda r: cam[i, r],
            lambda r: point[i, r],
            index[i],
            picked_from,
            pl.multiple_of(tile * SLOTS, SLOTS),
            None if first else rows,
            rows,
            put_to,
        )
        if first:
            for a in range(6):
                inverse_out[a, pl.ds(i, 1), :] = inverse[a]
        return total + term

    dot[...] += lax.fori_loop(0, block, advance, jnp.zeros(dot.shape, jnp.float32), unroll=True)

    @pl.when(step == pl.num_programs(0) - 1)
    def _():
        high, low = split_two(put_to[...])
        out[...] = jnp.dot(put[...], high, preferred_element_type=jnp.float32) + jnp.dot(
            put[...], low, preferred_element_type=jnp.float32
        )
        after()


def total_of(value):
    return jnp.sum(value, keepdims=True).reshape(1, 1)


def finish(place, damp, vector, out, dot):
    rows = damp.shape[0]
    own = pl.ds(pl.multiple_of(place[0] * rows, rows), rows)
    damped = damp[...] * vector[own, :]
    out[own, :] += damped
    part = total_of(dot[...]) + total_of(damped * vector[own, :])
    lane = lax.broadcasted_iota(jnp.int32, (out.shape[0], 128), 1)
    out[:, WIDTH - 128 :] += jnp.where(lane >= TILE - (WIDTH - 128), part, 0.0)


def first_kernel(ranks, counts, place, cam, point, index, extra, pick, put, damp, *refs):
    pieces, (out, inverse, residual, scaling, vector, energy, dot, picked_from, put_to) = refs[:ranks], refs[ranks:]

    def before():
        ring, _, rows, _ = pieces[0].shape
        for r in range(ranks):
            for away in range(ring):
                at = pl.multiple_of((r * ring + (away ^ place[0])) * rows, rows)
                residual[pl.ds(at, rows), :] = pieces[r][away, 0]
                scaling[pl.ds(at, rows), :] = pieces[r][away, 1]
        scaled = residual[...] * scaling[...]
        vector[...] = scaled
        energy[...] = jnp.broadcast_to(total_of(scaled * residual[...]), energy.shape)

    product_steps(
        counts, cam, point, index, extra, pick, put, vector, out, inverse, dot, picked_from, put_to, before,
        lambda: finish(place, damp, vector, out, dot),
    )


def next_kernel(ranks, counts, place, cam, point, index, extra, pick, put, damp, *refs):
    pieces = refs[:ranks]
    old_residual, scaling, old_vector, old_energy, old_answer = refs[ranks : ranks + 5]
    out, residual, vector, energy, answer, dot, picked_from, put_to = refs[ranks + 5 :]

    def before():
        many = pieces[0].shape[0]
        rows = damp.shape[0]
        step_size = old_energy[0:1, 0:1] / pieces[0][0:1, TILE : TILE + 1]
        own = pl.ds(pl.multiple_of(place[0] * rows, rows), rows)
        answer[...] = old_answer[...] + step_size * old_vector[own, :]
        power = jnp.zeros((1, 1), jnp.float32)
        for r in range(ranks):
            part = slice(r * many, (r + 1) * many)
            left = old_residual[part, :] - step_size * pieces[r][...]
            residual[part, :] = left
            scaled = scaling[part, :] * left
            vector[part, :] = scaled
            power = power + total_of(scaled * left)
        vector[...] += (power / old_energy[0:1, 0:1]) * old_vector[...]
        energy[...] = jnp.broadcast_to(power, energy.shape)

    product_steps(
        counts, cam, point, index, extra, pick, put, vector, out, None, dot, picked_from, put_to, before,
        lambda: finish(place, damp, vector, out, dot),
    )


def plain_kernel(counts, cam, point, index, extra, pick, put, vector, out, inverse, dot, picked_from, put_to):
    product_steps(
        counts, cam, point, index, extra, pick, put, vector, out, inverse, dot, picked_from, put_to,
        lambda: None, lambda: None,
    )


def last_kernel(place, piece, old_residual, old_vector, energy, old_answer, answer, residual):
    rows = old_answer.shape[0]
    step_size = energy[0:1, 0:1] / piece[0:1, TILE : TILE + 1]
    own = pl.ds(pl.multiple_of(place[0] * rows, rows), rows)
    answer[0] = (old_answer[...] + step_size * old_vector[own, :])[:, :TILE]
    residual[0] = (old_residual[own, :] - step_size * piece[own, :])[:, :TILE]


def whole(shape):
    return pl.BlockSpec(shape, lambda s, *refs: (0,) * len(shape))


def call_product(kernel, scalars, problem, extra, tables, others, outs):
    cam, point, index = problem
    tiles = cam.shape[0]
    block = BLOCK if tiles % BLOCK == 0 else tiles
    in_specs = [
        pl.BlockSpec((block,) + cam.shape[1:], lambda s, *refs: (s, 0, 0, 0)),
        pl.BlockSpec((block,) + point.shape[1:], lambda s, *refs: (s, 0, 0, 0)),
        pl.BlockSpec((block,) + index.shape[1:], lambda s, *refs: (s, 0, 0)),
        pl.BlockSpec((extra.shape[0], block, POINTS), lambda s, *refs: (0, s, 0)),
    ]
    in_specs += [whole(array.shape) for array in tables + others]
    out_specs = [
        pl.BlockSpec((shape[0], block, shape[2]), lambda s, *refs: (0, s, 0)) if split else whole(shape)
        for shape, split in outs
    ]
    scratch = pltpu.VMEM((tiles * SLOTS, WIDTH), jnp.float32)
    return pl.pallas_call(
        kernel,
        out_shape=[jax.ShapeDtypeStruct(shape, jnp.float32) for shape, split in outs],
        grid_spec=pltpu.PrefetchScalarGridSpec(
            num_scalar_prefetch=len(scalars),
            grid=(tiles // block,),
            in_specs=in_specs,
            out_specs=out_specs,
            scratch_shapes=[pltpu.VMEM((8, 128), jnp.float32), scratch, scratch],
        ),
        compiler_params=pltpu.CompilerParams(
            vmem_limit_bytes=32 * 2**20, dimension_semantics=("arbitrary",)
        ),
    )(*scalars, cam, point, index, extra, *tables, *others)


def tables_of(rows, window):
    listed = rows.reshape(-1)
    places = lax.iota(jnp.int32, window)
    pick = (listed[:, None] == places[None, :]).astype(jnp.bfloat16)
    put = (places[:, None] == listed[None, :]).astype(jnp.bfloat16)
    return [pick, put]


def widen(array):
    return jnp.pad(array, [(0, 0)] * (array.ndim - 1) + [(0, WIDTH - TILE)])


def exchange(array, mask):
    devices = lax.axis_size("pts") * lax.axis_size("cam")
    return lax.ppermute(array, AXES, [(i, i ^ mask) for i in range(devices)])


def two_groups(rhs, damp_cam, precond, problem, damp_point, tile_ids, counts):
    CAM, CORE, Y = 1, 2, 4
    shards = lax.axis_size("pts")
    tiles = rhs.shape[0]
    ring = shards // 4
    group, shard = lax.axis_index("cam"), lax.axis_index("pts")
    group_tiles = shards * tiles
    window = 2 * group_tiles
    place = (shard >> 2).reshape(1)
    where = (group * group_tiles + tile_ids - group_tiles // 2) % window
    owner_group, owner = where // group_tiles, where % group_tiles // tiles
    apart = owner ^ shard
    rank = (apart & 1) * 4 + (owner_group ^ group) * 2 + ((apart >> 1) & 1)
    tables = tables_of((rank * ring + (owner >> 2)) * tiles + where % tiles, window)
    scalars = [counts, place]
    damp = widen(damp_cam)

    def gather(own):
        near = [own, exchange(own, Y), exchange(own, CAM), exchange(own, CAM | Y)]
        return near + [exchange(piece, CORE) for piece in near]

    def reduce(partial):
        half = window // 2
        mine = partial[:half] + exchange(partial[half:], CORE)
        part = half // 4
        mine = (
            mine[:part]
            + exchange(mine[part : 2 * part], Y)
            + exchange(mine[2 * part : 3 * part], CAM)
            + exchange(mine[3 * part :], CAM | Y)
        )
        away = 1
        while away < ring:
            mine = mine + exchange(mine, 8 * away)
            away *= 2
        return mine

    both = widen(jnp.stack([rhs, precond]))[None]
    away = 1
    while away < ring:
        both = jnp.concatenate([both, exchange(both, 8 * away)], axis=0)
        away *= 2
    pieces = gather(both)
    full, small, own = (window, WIDTH), (8, 128), (tiles, WIDTH)
    inverse_shape = (6, problem[0].shape[0], POINTS)
    partial, inverse, residual, scaling, vector, energy = call_product(
        functools.partial(first_kernel, 8), scalars, problem, damp_point, tables, [damp] + pieces,
        [(full, 0), (inverse_shape, 1), (full, 0), (full, 0), (full, 0), (small, 0)],
    )
    answer = jnp.zeros(own, jnp.float32)
    for iteration in range(1, ITERS):
        pieces = gather(reduce(partial))
        partial, residual, vector, energy, answer = call_product(
            functools.partial(next_kernel, 8), scalars, problem, inverse, tables,
            [damp] + pieces + [residual, scaling, vector, energy, answer],
            [(full, 0), (full, 0), (full, 0), (small, 0), (own, 0)],
        )
    mine = reduce(partial)
    return pl.pallas_call(
        last_kernel,
        out_shape=[jax.ShapeDtypeStruct((1, tiles, TILE), jnp.float32)] * 2,
        in_specs=[pl.BlockSpec(memory_space=pltpu.SMEM)] + [pl.BlockSpec(memory_space=VMEM)] * 5,
    )(place, mine, residual[: mine.shape[0]], vector[: mine.shape[0]], energy, answer)


def from_behind(shard, axis, by):
    devices = lax.axis_size(axis)
    return lax.ppermute(shard, axis, [(i, (i + by) % devices) for i in range(devices)])


def many_groups(rhs, damp_cam, precond, problem, damp_point, tile_ids, counts):
    group_tiles = lax.axis_size("pts") * rhs.shape[0]
    halfway = group_tiles // 2
    window = 2 * group_tiles
    tables = tables_of(tile_ids, window)
    inverse_shape = (6, problem[0].shape[0], POINTS)

    def product(vector):
        panel = lax.all_gather(widen(vector), "pts", axis=0, tiled=True)
        lower = from_behind(panel[halfway:], "cam", 1)
        upper = from_behind(panel[:halfway], "cam", -1)
        whole_window = jnp.concatenate([lower, panel, upper], axis=0)
        partial = call_product(
            plain_kernel, [counts], problem, damp_point, tables, [whole_window],
            [((window, WIDTH), 0), (inverse_shape, 1)],
        )[0]
        from_above = from_behind(partial[:halfway], "cam", -1)
        from_below = from_behind(partial[halfway + group_tiles :], "cam", 1)
        summed = partial[halfway : halfway + group_tiles] + jnp.concatenate(
            [from_below, from_above], axis=0
        )
        return lax.psum_scatter(summed, "pts", scatter_dimension=0, tiled=True)[:, :TILE] + damp_cam * vector

    def inner(one, two):
        return lax.psum(jnp.sum(one * two), AXES)

    answer, residual = jnp.zeros(rhs.shape, jnp.float32), rhs
    scaled = precond * residual
    direction = scaled
    energy = inner(residual, scaled)
    for iteration in range(ITERS):
        mapped = product(direction)
        step_size = energy / inner(direction, mapped)
        answer = answer + step_size * direction
        residual = residual - step_size * mapped
        scaled = precond * residual
        energy_next = inner(residual, scaled)
        direction = scaled + energy_next / energy * direction
        energy = energy_next
    return answer[None], residual[None]


def on_device(rhs, damp_cam, precond, cam_jac, pt_jac, damp_pt, cam_index, tile_ids, counts):
    problem = (
        jnp.transpose(cam_jac[0], (0, 2, 1, 3)),
        jnp.transpose(pt_jac[0], (0, 2, 1, 3)),
        cam_index[0],
    )
    groups, shards = lax.axis_size("cam"), lax.axis_size("pts")
    plan = two_groups if groups == 2 and shards in (4, 8, 16, 32) else many_groups
    outputs = plan(
        rhs[0], damp_cam[0], precond[0], problem, jnp.transpose(damp_pt[0], (1, 0, 2)), tile_ids[0], counts[0]
    )
    return tuple(outputs)


def solution(mesh):
    return jax.shard_map(
        on_device,
        mesh=mesh,
        in_specs=(
            P("cam", "pts", None),
            P("cam", "pts", None),
            P("cam", "pts", None),
            P("cam", "pts", None, None, None),
            P("cam", "pts", None, None, None),
            P("cam", "pts", None, None),
            P("cam", "pts", None, None),
            P("cam", "pts", None),
            P("cam", "pts"),
        ),
        out_specs=(P("cam", "pts", None), P("cam", "pts", None)),
        check_vma=False,
    )
```

```python
import functools
import math

import jax
import jax.numpy as jnp
from jax import lax
from jax.experimental import pallas as pl
from jax.experimental.pallas import tpu as pltpu
from jax.sharding import PartitionSpec as P

ITERS = 3
CPAR = 9
CAMERAS = 64
SLOTS = 8
POINTS = 128
TILE = CPAR * CAMERAS
PAIRS = 5
WIDTH = PAIRS * 128
BATCH = 96
AXES = ("pts", "cam")


def split_two(value):
    high = value.astype(jnp.bfloat16)
    low = (value - high.astype(jnp.float32)).astype(jnp.bfloat16)
    return high, low


def all_slots(value):
    for by in (4, 2, 1):
        value = value + pltpu.roll(value, by, 0)
    return value


def invert(gram):
    a, b, c, d, e, f = gram
    aa = d * f - e * e
    bb = c * e - b * f
    cc = b * e - c * d
    dd = a * f - c * c
    ee = b * c - a * e
    ff = a * d - b * b
    scale = 1.0 / (a * aa + b * bb + c * cc)
    return [entry * scale for entry in (aa, bb, cc, dd, ee, ff)]


def setup_kernel(counts, cam, point, index, damp, cam_out, point_out, index_out, inverse_out, selector_out):
    step = pl.program_id(0)
    block = cam.shape[0]
    slot = lax.broadcasted_iota(jnp.int32, (SLOTS, POINTS), 0)
    camera = lax.broadcasted_iota(jnp.int32, (CAMERAS, POINTS), 0).astype(jnp.bfloat16)
    one = jnp.ones((CAMERAS, POINTS), jnp.bfloat16)
    zero = jnp.zeros((CAMERAS, POINTS), jnp.bfloat16)

    def advance(i, carry):
        live = (slot < counts[step * block + i]).astype(jnp.float32)
        for r in range(2 * CPAR):
            cam_out[i, r] = cam[i, r] * live
        rows = [point[i, r] for r in range(6)]
        for r in range(6):
            point_out[i, r] = rows[r]
        seen = index[i]
        index_out[i] = seen
        rows = [row * live for row in rows]
        entries = [(0, 0), (0, 1), (0, 2), (1, 1), (1, 2), (2, 2)]
        gram = [all_slots(rows[a] * rows[b] + rows[3 + a] * rows[3 + b]) for a, b in entries]
        for a, entry in enumerate((0, 3, 5)):
            gram[entry] = gram[entry] + damp[a, pl.ds(i, 1), :]
        for a, entry in enumerate(invert(gram)):
            inverse_out[i, a] = entry
        wide = seen.astype(jnp.float32)
        for k in range(SLOTS):
            row = wide[k : k + 1, :].astype(jnp.bfloat16)
            down, right = k // 2 * CAMERAS, k % 2 * POINTS
            selector_out[i, down : down + CAMERAS, right : right + POINTS] = jnp.where(camera == row, one, zero)
        return carry

    lax.fori_loop(0, block, advance, 0, unroll=4)


def tile_product(cam, point, index, inverse, selector, picked_from, row, put_to):
    slot = lax.broadcasted_iota(jnp.int32, (SLOTS, POINTS), 0)
    lane = lax.broadcasted_iota(jnp.int32, (SLOTS, POINTS), 1)
    other = index + CAMERAS
    pairs = [picked_from[pl.ds(row, SLOTS), p * 128 : (p + 1) * 128] for p in range(PAIRS)]
    picked = [
        jnp.take_along_axis(
            pairs[j // 2], other if j % 2 else index, axis=1, mode="promise_in_bounds"
        )
        for j in range(CPAR)
    ]
    rows = [point(r) for r in range(6)]
    q = []
    for r in range(2):
        total = cam(9 * r) * picked[0]
        for j in range(1, CPAR):
            total = total + cam(9 * r + j) * picked[j]
        q.append(total)
    y = [all_slots(rows[a] * q[0] + rows[3 + a] * q[1]) for a in range(3)]
    i0, i1, i2, i3, i4, i5 = [inverse(a) for a in range(6)]
    z = [
        i0 * y[0] + i1 * y[1] + i2 * y[2],
        i1 * y[0] + i3 * y[1] + i4 * y[2],
        i2 * y[0] + i4 * y[1] + i5 * y[2],
    ]
    e = [
        q[r] - (rows[3 * r] * z[0] + rows[3 * r + 1] * z[1] + rows[3 * r + 2] * z[2])
        for r in range(2)
    ]
    slot_twice = lax.broadcasted_iota(jnp.int32, (2 * SLOTS, POINTS), 0) & 1
    odd = slot_twice.astype(jnp.bfloat16)
    even = (1 - slot_twice).astype(jnp.bfloat16)
    left = []
    for j in range(CPAR):
        returned = cam(j) * e[0] + cam(9 + j) * e[1]
        high = returned.astype(jnp.bfloat16).astype(jnp.float32)
        both = jnp.concatenate([high, returned - high], axis=0).astype(jnp.bfloat16)
        left.append(jnp.concatenate([both * even, both * odd], axis=1))
    left = jnp.concatenate(left, axis=0)
    spread = lax.dot_general(
        left, selector, (((1,), (1,)), ((), ())), preferred_element_type=jnp.float32
    )
    side = (slot >> 1) & 1
    first_side = side == 0
    keep = (lane >> 6) == side
    sums = []
    for j in range(CPAR):
        both = spread[16 * j : 16 * j + 8] + spread[16 * j + 8 : 16 * j + 16]
        sums.append(jnp.where(slot < 4, both[:, :128], both[:, 128:]))
    sums.append(jnp.zeros_like(sums[0]))
    for p in range(PAIRS):
        one, two = sums[2 * p], sums[2 * p + 1]
        stay = jnp.where(first_side, one, two)
        move = pltpu.roll(jnp.where(first_side, two, one), CAMERAS, 1)
        put_to[pl.ds(row, SLOTS), p * 128 : (p + 1) * 128] = jnp.where(keep, stay, move)
    return q[0] * e[0] + q[1] * e[1]


def product_steps(problem, pick, put, vector, out, picked_from, put_to):
    cam, point, index, inverse, selector = problem
    tiles = cam.shape[0]
    batch = math.gcd(tiles, BATCH)
    high, low = split_two(vector[...])
    picked_from[...] = jnp.dot(
        pick[...], high, preferred_element_type=jnp.float32
    ) + jnp.dot(pick[...], low, preferred_element_type=jnp.float32)

    def advance(step, total):
        for turn in range(batch):
            i = step * batch + turn
            total = total + tile_product(
                lambda r: cam[i, r],
                lambda r: point[i, r],
                index[i],
                lambda a: inverse[i, a],
                selector[i],
                picked_from,
                pl.multiple_of(i * SLOTS, SLOTS),
                put_to,
            )
        return total

    dot = lax.fori_loop(0, tiles // batch, advance, jnp.zeros((SLOTS, POINTS), jnp.float32))
    high, low = split_two(put_to[...])
    out[...] = jnp.dot(put[...], high, preferred_element_type=jnp.float32) + jnp.dot(
        put[...], low, preferred_element_type=jnp.float32
    )
    return dot


def total_of(value):
    return jnp.sum(value, keepdims=True).reshape(1, 1)


def finish(place, damp, vector, out, dot):
    rows = damp.shape[0]
    own = pl.ds(pl.multiple_of(place[0] * rows, rows), rows)
    damped = damp[...] * vector[own, :]
    out[own, :] += damped
    part = total_of(dot) + total_of(damped * vector[own, :])
    lane = lax.broadcasted_iota(jnp.int32, (out.shape[0], 128), 1)
    out[:, WIDTH - 128 :] += jnp.where(lane >= TILE - (WIDTH - 128), part, 0.0)


def first_kernel(ranks, place, *refs):
    problem, (pick, put, damp), refs = refs[:5], refs[5:8], refs[8:]
    pieces, refs = refs[:ranks], refs[ranks:]
    out, residual, scaling, vector, energy, picked_from, put_to = refs
    ring, _, rows, _ = pieces[0].shape
    for r in range(ranks):
        for away in range(ring):
            at = pl.multiple_of((r * ring + (away ^ place[0])) * rows, rows)
            residual[pl.ds(at, rows), :] = pieces[r][away, 0]
            scaling[pl.ds(at, rows), :] = pieces[r][away, 1]
    scaled = residual[...] * scaling[...]
    vector[...] = scaled
    energy[...] = jnp.broadcast_to(total_of(scaled * residual[...]), energy.shape)
    dot = product_steps(problem, pick, put, vector, out, picked_from, put_to)
    finish(place, damp, vector, out, dot)


def next_kernel(ranks, place, *refs):
    problem, (pick, put, damp), refs = refs[:5], refs[5:8], refs[8:]
    pieces, refs = refs[:ranks], refs[ranks:]
    old_residual, scaling, old_vector, old_energy, old_answer = refs[:5]
    out, residual, vector, energy, answer, picked_from, put_to = refs[5:]
    many = pieces[0].shape[0]
    rows = damp.shape[0]
    step_size = old_energy[0:1, 0:1] / pieces[0][0:1, TILE : TILE + 1]
    own = pl.ds(pl.multiple_of(place[0] * rows, rows), rows)
    answer[...] = old_answer[...] + step_size * old_vector[own, :]
    power = jnp.zeros((1, 1), jnp.float32)
    for r in range(ranks):
        part = slice(r * many, (r + 1) * many)
        left = old_residual[part, :] - step_size * pieces[r][...]
        residual[part, :] = left
        scaled = scaling[part, :] * left
        vector[part, :] = scaled
        power = power + total_of(scaled * left)
    vector[...] += (power / old_energy[0:1, 0:1]) * old_vector[...]
    energy[...] = jnp.broadcast_to(power, energy.shape)
    dot = product_steps(problem, pick, put, vector, out, picked_from, put_to)
    finish(place, damp, vector, out, dot)


def plain_kernel(*refs):
    problem, (pick, put, vector), (out, picked_from, put_to) = refs[:5], refs[5:8], refs[8:]
    product_steps(problem, pick, put, vector, out, picked_from, put_to)


def last_kernel(place, piece, old_residual, old_vector, energy, old_answer, answer, residual):
    rows = old_answer.shape[0]
    step_size = energy[0:1, 0:1] / piece[0:1, TILE : TILE + 1]
    own = pl.ds(pl.multiple_of(place[0] * rows, rows), rows)
    answer[0] = (old_answer[...] + step_size * old_vector[own, :])[:, :TILE]
    residual[0] = (old_residual[own, :] - step_size * piece[own, :])[:, :TILE]


def whole(shape):
    return pl.BlockSpec(shape, lambda s, *refs: (0,) * len(shape))


def by_tiles(block, shape):
    return pl.BlockSpec((block,) + shape[1:], lambda s, *refs: (s,) + (0,) * (len(shape) - 1))


def call_setup(counts, cam, point, index, damp):
    tiles = cam.shape[0]
    block = math.gcd(tiles, 16)
    shapes = [cam.shape, point.shape, index.shape, (tiles, 6, SLOTS, POINTS)]
    shapes += [(tiles, SLOTS // 2 * CAMERAS, 2 * POINTS)]
    kinds = [jnp.float32, jnp.float32, jnp.int32, jnp.float32, jnp.bfloat16]
    return pl.pallas_call(
        setup_kernel,
        out_shape=[pltpu.VMEM(shape, kind) for shape, kind in zip(shapes, kinds)],
        grid_spec=pltpu.PrefetchScalarGridSpec(
            num_scalar_prefetch=1,
            grid=(tiles // block,),
            in_specs=[by_tiles(block, shape) for shape in shapes[:3]]
            + [pl.BlockSpec((3, block, POINTS), lambda s, *refs: (0, s, 0))],
            out_specs=[by_tiles(block, shape) for shape in shapes],
        ),
        compiler_params=pltpu.CompilerParams(
            vmem_limit_bytes=14 * 2**20, dimension_semantics=("arbitrary",)
        ),
        cost_estimate=pl.CostEstimate(flops=10**8, bytes_accessed=3 * 10**7, transcendentals=0),
    )(counts, *[pltpu.with_memory_space_constraint(x, pltpu.HBM) for x in (cam, point, index, damp)])


def call_product(kernel, scalars, problem, others, outs):
    tiles = problem[0].shape[0]
    scratch = pltpu.VMEM((tiles * SLOTS, WIDTH), jnp.float32)
    held = [pltpu.with_memory_space_constraint(array, pltpu.VMEM) for array in problem]
    return pl.pallas_call(
        kernel,
        out_shape=[jax.ShapeDtypeStruct(shape, jnp.float32) for shape in outs],
        in_specs=[pl.BlockSpec(memory_space=pltpu.SMEM)] * len(scalars)
        + [pl.BlockSpec(memory_space=pltpu.VMEM)] * (len(held) + len(others)),
        out_specs=[pl.BlockSpec(memory_space=pltpu.VMEM)] * len(outs),
        scratch_shapes=[scratch, scratch],
        compiler_params=pltpu.CompilerParams(vmem_limit_bytes=20 * 2**20),
    )(*scalars, *held, *others)


def tables_of(rows, window):
    listed = rows.reshape(-1)
    places = lax.iota(jnp.int32, window)
    pick = (listed[:, None] == places[None, :]).astype(jnp.bfloat16)
    put = (places[:, None] == listed[None, :]).astype(jnp.bfloat16)
    return [pick, put]


def widen(array):
    return jnp.pad(array, [(0, 0)] * (array.ndim - 1) + [(0, WIDTH - TILE)])


def exchange(array, mask):
    devices = lax.axis_size("pts") * lax.axis_size("cam")
    return lax.ppermute(array, AXES, [(i, i ^ mask) for i in range(devices)])


def two_groups(rhs, damp_cam, precond, problem, tile_ids):
    CAM, CORE, Y, Z = 1, 2, 4, 8
    shards = lax.axis_size("pts")
    tiles = rhs.shape[0]
    ring = shards // 4
    group, shard = lax.axis_index("cam"), lax.axis_index("pts")
    group_tiles = shards * tiles
    window = 2 * group_tiles
    place = (shard >> 2).reshape(1)
    where = (group * group_tiles + tile_ids - group_tiles // 2) % window
    owner_group, owner = where // group_tiles, where % group_tiles // tiles
    apart = owner ^ shard
    rank = (apart & 1) * 4 + (owner_group ^ group) * 2 + ((apart >> 1) & 1)
    tables = tables_of((rank * ring + (owner >> 2)) * tiles + where % tiles, window)
    steady = tables + [widen(damp_cam)]

    def gather(own):
        near = [own, exchange(own, Y), exchange(own, CAM), exchange(own, CAM | Y)]
        return near + [exchange(piece, CORE) for piece in near]

    def reduce(partial):
        half = window // 2
        mine = partial[:half] + exchange(partial[half:], CORE)
        part = half // 4
        mine = (
            mine[:part]
            + exchange(mine[part : 2 * part], Y)
            + exchange(mine[2 * part : 3 * part], CAM)
            + exchange(mine[3 * part :], CAM | Y)
        )
        return sum([exchange(mine, Z * away) for away in range(1, ring)], mine)

    both = widen(jnp.stack([rhs, precond]))
    pieces = gather(jnp.stack([both] + [exchange(both, Z * away) for away in range(1, ring)]))
    full, small, own = (window, WIDTH), (8, 128), (tiles, WIDTH)
    partial, residual, scaling, vector, energy = call_product(
        functools.partial(first_kernel, 8), [place], problem, steady + pieces,
        [full, full, full, full, small],
    )
    answer = jnp.zeros(own, jnp.float32)
    for iteration in range(1, ITERS):
        pieces = gather(reduce(partial))
        partial, residual, vector, energy, answer = call_product(
            functools.partial(next_kernel, 8), [place], problem,
            steady + pieces + [residual, scaling, vector, energy, answer],
            [full, full, full, small, own],
        )
    mine = reduce(partial)
    return pl.pallas_call(
        last_kernel,
        out_shape=[jax.ShapeDtypeStruct((1, tiles, TILE), jnp.float32)] * 2,
        grid=(1,),
        in_specs=[pl.BlockSpec(memory_space=pltpu.SMEM)]
        + [whole(shape) for shape in (mine.shape, mine.shape, mine.shape, small, own)],
        out_specs=[whole((1, tiles, TILE))] * 2,
    )(place, mine, residual, vector, energy, answer)


def from_behind(shard, axis, by):
    devices = lax.axis_size(axis)
    return lax.ppermute(shard, axis, [(i, (i + by) % devices) for i in range(devices)])


def many_groups(rhs, damp_cam, precond, problem, tile_ids):
    group_tiles = lax.axis_size("pts") * rhs.shape[0]
    halfway = group_tiles // 2
    window = 2 * group_tiles
    tables = tables_of(tile_ids, window)

    def product(vector):
        panel = lax.all_gather(widen(vector), "pts", axis=0, tiled=True)
        lower = from_behind(panel[halfway:], "cam", 1)
        upper = from_behind(panel[:halfway], "cam", -1)
        whole_window = jnp.concatenate([lower, panel, upper], axis=0)
        partial = call_product(
            plain_kernel, [], problem, tables + [whole_window], [(window, WIDTH)]
        )[0]
        from_above = from_behind(partial[:halfway], "cam", -1)
        from_below = from_behind(partial[halfway + group_tiles :], "cam", 1)
        summed = partial[halfway : halfway + group_tiles] + jnp.concatenate(
            [from_below, from_above], axis=0
        )
        return lax.psum_scatter(summed, "pts", scatter_dimension=0, tiled=True)[:, :TILE] + damp_cam * vector

    def inner(one, two):
        return lax.psum(jnp.sum(one * two), AXES)

    answer, residual = jnp.zeros(rhs.shape, jnp.float32), rhs
    scaled = precond * residual
    direction = scaled
    energy = inner(residual, scaled)
    for iteration in range(ITERS):
        mapped = product(direction)
        step_size = energy / inner(direction, mapped)
        answer = answer + step_size * direction
        residual = residual - step_size * mapped
        scaled = precond * residual
        energy_next = inner(residual, scaled)
        direction = scaled + energy_next / energy * direction
        energy = energy_next
    return answer[None], residual[None]


def on_device(rhs, damp_cam, precond, cam_jac, pt_jac, damp_pt, cam_index, tile_ids, counts):
    problem = call_setup(
        counts[0],
        jnp.transpose(cam_jac[0], (0, 2, 1, 3)),
        jnp.transpose(pt_jac[0], (0, 2, 1, 3)),
        cam_index[0],
        jnp.transpose(damp_pt[0], (1, 0, 2)),
    )
    groups, shards = lax.axis_size("cam"), lax.axis_size("pts")
    plan = two_groups if groups == 2 and shards in (4, 8, 16, 32) else many_groups
    return tuple(plan(rhs[0], damp_cam[0], precond[0], problem, tile_ids[0]))


def solution(mesh):
    return jax.shard_map(
        on_device,
        mesh=mesh,
        in_specs=(
            P("cam", "pts", None),
            P("cam", "pts", None),
            P("cam", "pts", None),
            P("cam", "pts", None, None, None),
            P("cam", "pts", None, None, None),
            P("cam", "pts", None, None),
            P("cam", "pts", None, None),
            P("cam", "pts", None),
            P("cam", "pts"),
        ),
        out_specs=(P("cam", "pts", None), P("cam", "pts", None)),
        check_vma=False,
    )
```

```python
import functools
import math

import jax
import jax.numpy as jnp
from jax import lax
from jax.experimental import pallas as pl
from jax.experimental.pallas import tpu as pltpu
from jax.sharding import PartitionSpec as P

ITERS = 3
CPAR = 9
CAMERAS = 64
SLOTS = 8
POINTS = 128
TILE = CPAR * CAMERAS
PAIRS = 5
WIDTH = PAIRS * 128
CHUNKS = 2
AXES = ("pts", "cam")


def split_two(value):
    high = value.astype(jnp.bfloat16)
    low = (value - high.astype(jnp.float32)).astype(jnp.bfloat16)
    return high, low


def all_slots(value):
    for by in (4, 2, 1):
        value = value + pltpu.roll(value, by, 0)
    return value


def invert(gram):
    a, b, c, d, e, f = gram
    aa = d * f - e * e
    bb = c * e - b * f
    cc = b * e - c * d
    dd = a * f - c * c
    ee = b * c - a * e
    ff = a * d - b * b
    scale = 1.0 / (a * aa + b * bb + c * cc)
    return [entry * scale for entry in (aa, bb, cc, dd, ee, ff)]


def setup_kernel(
    skip, group, counts, cam, point, index, damp,
    cam_out, point_out, index_out, inverse_out, selector_out, damping, arrived,
):
    tiles = cam_out.shape[0]
    turns = tiles // group

    def copy(array, out, turn, kind):
        here = pl.ds(turn * group, group)
        there = pl.ds(skip + turn * group, group)
        return pltpu.make_async_copy(array.at[there], out.at[here], arrived.at[kind, turn])

    damping_copy = pltpu.make_async_copy(damp.at[:, pl.ds(skip, tiles)], damping, arrived.at[3, 0])
    damping_copy.start()
    for kind, (array, out) in enumerate(((point, point_out), (index, index_out), (cam, cam_out))):
        for turn in range(turns):
            copy(array, out, turn, kind).start()
    slot = lax.broadcasted_iota(jnp.int32, (SLOTS, POINTS), 0)
    camera = lax.broadcasted_iota(jnp.int32, (CAMERAS, POINTS), 0).astype(jnp.bfloat16)
    one = jnp.ones((CAMERAS, POINTS), jnp.bfloat16)
    zero = jnp.zeros((CAMERAS, POINTS), jnp.bfloat16)
    damping_copy.wait()
    for turn in range(turns):
        copy(point, point_out, turn, 0).wait()
        copy(index, index_out, turn, 1).wait()
        for i in range(turn * group, (turn + 1) * group):
            live = (slot < counts[skip + i]).astype(jnp.float32)
            rows = [point_out[i, r] * live for r in range(6)]
            entries = [(0, 0), (0, 1), (0, 2), (1, 1), (1, 2), (2, 2)]
            gram = [all_slots(rows[a] * rows[b] + rows[3 + a] * rows[3 + b]) for a, b in entries]
            for a, entry in enumerate((0, 3, 5)):
                gram[entry] = gram[entry] + damping[a, i : i + 1, :]
            for a, entry in enumerate(invert(gram)):
                inverse_out[i, a] = entry
            wide = index_out[i].astype(jnp.float32)
            for k in range(SLOTS):
                row = wide[k : k + 1, :].astype(jnp.bfloat16)
                down, right = k // 2 * CAMERAS, k % 2 * POINTS
                selector_out[i, down : down + CAMERAS, right : right + POINTS] = jnp.where(
                    camera == row, one, zero
                )
    for turn in range(turns):
        copy(cam, cam_out, turn, 2).wait()


def tile_product(cam, point, index, inverse, selector, picked_from, row, put_to):
    slot = lax.broadcasted_iota(jnp.int32, (SLOTS, POINTS), 0)
    lane = lax.broadcasted_iota(jnp.int32, (SLOTS, POINTS), 1)
    other = index + CAMERAS
    pairs = [picked_from[pl.ds(row, SLOTS), p * 128 : (p + 1) * 128] for p in range(PAIRS)]
    picked = [
        jnp.take_along_axis(
            pairs[j // 2], other if j % 2 else index, axis=1, mode="promise_in_bounds"
        )
        for j in range(CPAR)
    ]
    rows = [point(r) for r in range(6)]
    q = []
    for r in range(2):
        total = cam(9 * r) * picked[0]
        for j in range(1, CPAR):
            total = total + cam(9 * r + j) * picked[j]
        q.append(total)
    y = [all_slots(rows[a] * q[0] + rows[3 + a] * q[1]) for a in range(3)]
    i0, i1, i2, i3, i4, i5 = [inverse(a) for a in range(6)]
    z = [
        i0 * y[0] + i1 * y[1] + i2 * y[2],
        i1 * y[0] + i3 * y[1] + i4 * y[2],
        i2 * y[0] + i4 * y[1] + i5 * y[2],
    ]
    e = [
        q[r] - (rows[3 * r] * z[0] + rows[3 * r + 1] * z[1] + rows[3 * r + 2] * z[2])
        for r in range(2)
    ]
    slot_twice = lax.broadcasted_iota(jnp.int32, (2 * SLOTS, POINTS), 0) & 1
    odd = slot_twice.astype(jnp.bfloat16)
    even = (1 - slot_twice).astype(jnp.bfloat16)
    returned = [cam(j) * e[0] + cam(9 + j) * e[1] for j in range(CPAR)]
    left = []
    for p in range(PAIRS - 1):
        left += split_two(jnp.concatenate(returned[2 * p : 2 * p + 2], axis=0))
    high = returned[-1].astype(jnp.bfloat16).astype(jnp.float32)
    left.append(jnp.concatenate([high, returned[-1] - high], axis=0).astype(jnp.bfloat16))
    left = jnp.concatenate(
        [jnp.concatenate([rows * even, rows * odd], axis=1) for rows in left], axis=0
    )
    spread = lax.dot_general(
        left, selector, (((1,), (1,)), ((), ())), preferred_element_type=jnp.float32
    )
    side = (slot >> 1) & 1
    first_side = side == 0
    keep = (lane >> 6) == side
    sums = []
    for j in range(CPAR):
        first = 32 * (j // 2) + 8 * (j % 2)
        second = first + (16 if j < CPAR - 1 else 8)
        both = spread[first : first + 8] + spread[second : second + 8]
        sums.append(jnp.where(slot < 4, both[:, :128], both[:, 128:]))
    sums.append(jnp.zeros_like(sums[0]))
    for p in range(PAIRS):
        one, two = sums[2 * p], sums[2 * p + 1]
        stay = jnp.where(first_side, one, two)
        move = pltpu.roll(jnp.where(first_side, two, one), CAMERAS, 1)
        put_to[pl.ds(row, SLOTS), p * 128 : (p + 1) * 128] = jnp.where(keep, stay, move)
    return q[0] * e[0] + q[1] * e[1]


def wide_dot(table, value):
    both = jnp.dot(
        table, jnp.concatenate(split_two(value), axis=1), preferred_element_type=jnp.float32
    )
    return both[:, :WIDTH] + both[:, WIDTH:]


def product_steps(problem, pick, put, vector, out, picked_from, put_to):
    picked_from[...] = wide_dot(pick[...], vector[...])
    total = jnp.zeros((SLOTS, POINTS), jnp.float32)
    row = 0
    for cam, point, index, inverse, selector in problem:
        for i in range(cam.shape[0]):
            total = total + tile_product(
                lambda r: cam[i, r],
                lambda r: point[i, r],
                index[i],
                lambda a: inverse[i, a],
                selector[i],
                picked_from,
                row,
                put_to,
            )
            row += SLOTS
    out[...] = wide_dot(put[...], put_to[...])
    return total


def total_of(value):
    return jnp.sum(value, keepdims=True).reshape(1, 1)


def in_spare(rows, value):
    lane = lax.broadcasted_iota(jnp.int32, (rows, 128), 1)
    return jnp.where(lane >= TILE - (WIDTH - 128), value, 0.0)


def spare_of(ref):
    return ref[0:1, TILE : TILE + 1]


def offer(residual, scaling, scaled):
    value = scaling[...] * residual[...]
    scaled[...] = value
    part = total_of(value * residual[...])
    scaled[:, WIDTH - 128 :] += in_spare(scaled.shape[0], part)


def start_kernel(*refs):
    pieces, (residual, scaling, scaled) = refs[:-4], refs[-3:]
    rows = pieces[0].shape[1]
    for away, piece in enumerate(pieces):
        residual[away * rows : (away + 1) * rows, :] = piece[0]
        scaling[away * rows : (away + 1) * rows, :] = piece[1]
    offer(residual, scaling, scaled)


def turn_kernel(ring, *refs):
    pieces, refs = refs[:ring], refs[ring:]
    energy, vector, old_answer, old_residual, scaling, answer, residual, scaled = refs
    rows = answer.shape[0]
    step_size = energy[0:1, 0:1] / sum([spare_of(piece) for piece in pieces])
    for b in range(ring):
        here = slice(b * rows, (b + 1) * rows)
        mapped = pieces[0][here, :]
        for a in range(1, ring):
            mapped = mapped + pieces[a][(a ^ b) * rows : ((a ^ b) + 1) * rows, :]
        residual[here, :] = old_residual[here, :] - step_size * mapped
    answer[...] = old_answer[...] + step_size * vector[:rows, :]
    offer(residual, scaling, scaled)


def last_kernel(ring, *refs):
    pieces, (energy, vector, old_answer, old_residual, answer, residual) = refs[:ring], refs[ring:]
    rows = old_answer.shape[0]
    mapped = sum([piece[...] for piece in pieces[1:]], pieces[0][...])
    step_size = energy[0:1, 0:1] / mapped[0:1, TILE : TILE + 1]
    answer[0] = (old_answer[...] + step_size * vector[:rows, :])[:, :TILE]
    residual[0] = (old_residual[:rows, :] - step_size * mapped)[:, :TILE]


def step_kernel(chunks, ranks, first, *refs):
    problem = [refs[5 * c : 5 * c + 5] for c in range(chunks)]
    (pick, put, damp), refs = refs[5 * chunks : 5 * chunks + 3], refs[5 * chunks + 3 :]
    pieces, refs = refs[:ranks], refs[ranks:]
    if not first:
        (old_vector, old_energy), refs = refs[:2], refs[2:]
    out, vector, energy, picked_from, put_to = refs
    power = sum([spare_of(piece) for piece in pieces])
    energy[...] = jnp.broadcast_to(power, energy.shape)
    many = pieces[0].shape[0]
    for r in range(ranks):
        part = slice(r * many, (r + 1) * many)
        if first:
            vector[part, :] = pieces[r][...]
        else:
            vector[part, :] = pieces[r][...] + (power / old_energy[0:1, 0:1]) * old_vector[part, :]
    dot = product_steps(problem, pick, put, vector, out, picked_from, put_to)
    rows = damp.shape[0]
    damped = damp[...] * vector[:rows, :]
    out[:rows, :] += damped
    out[:, WIDTH - 128 :] += in_spare(out.shape[0], total_of(dot) + total_of(damped * vector[:rows, :]))


def plain_kernel(chunks, *refs):
    problem = [refs[5 * c : 5 * c + 5] for c in range(chunks)]
    pick, put, vector, out, picked_from, put_to = refs[5 * chunks :]
    product_steps(problem, pick, put, vector, out, picked_from, put_to)


def in_vmem(kernel, operands, outs, scratch=()):
    spec = pl.BlockSpec(memory_space=pltpu.VMEM)
    return pl.pallas_call(
        kernel,
        out_shape=[jax.ShapeDtypeStruct(shape, jnp.float32) for shape in outs],
        in_specs=[spec] * len(operands),
        out_specs=[spec] * len(outs),
        scratch_shapes=list(scratch),
        compiler_params=pltpu.CompilerParams(vmem_limit_bytes=20 * 2**20),
    )(*operands)


def call_setup(skip, tiles, counts, cam, point, index, damp):
    group = math.gcd(tiles, 8)
    shapes = [(tiles,) + array.shape[1:] for array in (cam, point, index)]
    shapes += [(tiles, 6, SLOTS, POINTS), (tiles, SLOTS // 2 * CAMERAS, 2 * POINTS)]
    kinds = [jnp.float32, jnp.float32, jnp.int32, jnp.float32, jnp.bfloat16]
    return pl.pallas_call(
        functools.partial(setup_kernel, skip, group),
        out_shape=[pltpu.VMEM(shape, kind) for shape, kind in zip(shapes, kinds)],
        in_specs=[pl.BlockSpec(memory_space=pltpu.SMEM)] + [pl.BlockSpec(memory_space=pltpu.HBM)] * 4,
        out_specs=[pl.BlockSpec(memory_space=pltpu.VMEM)] * 5,
        scratch_shapes=[
            pltpu.VMEM((3, tiles, POINTS), jnp.float32),
            pltpu.SemaphoreType.DMA((4, tiles // group)),
        ],
        compiler_params=pltpu.CompilerParams(vmem_limit_bytes=4 * 2**20),
        cost_estimate=pl.CostEstimate(flops=3 * 10**7, bytes_accessed=10**7, transcendentals=0),
    )(counts, *[pltpu.with_memory_space_constraint(x, pltpu.HBM) for x in (cam, point, index, damp)])


def call_product(kernel, problem, others, outs):
    tiles = sum(chunk[0].shape[0] for chunk in problem)
    scratch = pltpu.VMEM((tiles * SLOTS, WIDTH), jnp.float32)
    held = [pltpu.with_memory_space_constraint(array, pltpu.VMEM) for chunk in problem for array in chunk]
    return in_vmem(kernel, held + others, outs, [scratch, scratch])


def tables_of(rows, counts, window):
    live = lax.iota(jnp.int32, SLOTS)[None, :] < counts[:, None]
    listed = jnp.where(live, rows, -1).reshape(-1)
    places = lax.iota(jnp.int32, window)
    pick = (listed[:, None] == places[None, :]).astype(jnp.bfloat16)
    put = (places[:, None] == listed[None, :]).astype(jnp.bfloat16)
    return [pick, put]


def widen(array):
    return jnp.pad(array, [(0, 0)] * (array.ndim - 1) + [(0, WIDTH - TILE)])


def exchange(array, mask):
    devices = lax.axis_size("pts") * lax.axis_size("cam")
    return lax.ppermute(array, AXES, [(i, i ^ mask) for i in range(devices)])


def two_groups(rhs, damp_cam, precond, problem, tile_ids, counts):
    CAM, CORE, Y, Z = 1, 2, 4, 8
    shards = lax.axis_size("pts")
    tiles = rhs.shape[0]
    ring = shards // 4
    group, shard = lax.axis_index("cam"), lax.axis_index("pts")
    group_tiles = shards * tiles
    window = 2 * group_tiles
    where = (group * group_tiles + tile_ids - group_tiles // 2) % window
    owner_group, owner = where // group_tiles, where % group_tiles // tiles
    apart = owner ^ shard
    rank = (apart & 1) * 4 + (owner_group ^ group) * 2 + ((apart >> 1) & 1)
    tables = tables_of((rank * ring + (apart >> 2)) * tiles + where % tiles, counts, window)
    steady = tables + [widen(damp_cam)]

    def gather(own, ahead=None):
        near = [own, exchange(own, Y), exchange(own, CAM), exchange(own, CAM | Y)]
        if ahead is not None:
            near = list(lax.optimization_barrier((*near, ahead)))[:4]
        return near + [exchange(piece, CORE) for piece in near]

    def reduce(partial):
        half = window // 2
        mine = partial[:half] + exchange(partial[half:], CORE)
        part = half // 4
        return (
            mine[:part]
            + exchange(mine[part : 2 * part], Y)
            + exchange(mine[2 * part : 3 * part], CAM)
            + exchange(mine[3 * part :], CAM | Y)
        )

    full, line, small, own = (window, WIDTH), (ring * tiles, WIDTH), (8, 128), (tiles, WIDTH)
    both = widen(jnp.stack([rhs, precond]))
    both = [both] + [exchange(both, Z * away) for away in range(1, ring)]
    residual, scaling, scaled = in_vmem(start_kernel, both + [problem[0][2]], [line, line, line])
    answer = jnp.zeros(own, jnp.float32)
    known = []
    for iteration in range(ITERS):
        partial, vector, energy = call_product(
            functools.partial(step_kernel, len(problem), 8, iteration == 0),
            problem, steady + gather(scaled, problem[-1][2] if iteration == 0 else None) + known, [full, full, small],
        )
        known = [vector, energy]
        mine = reduce(partial)
        if iteration + 1 < ITERS:
            parts = [mine] + [exchange(mine, Z * away) for away in range(1, ring)]
            answer, residual, scaled = in_vmem(
                functools.partial(turn_kernel, ring),
                parts + [energy, vector, answer, residual, scaling],
                [own, line, line],
            )
    parts = [mine[:tiles]] + [
        exchange(mine[away * tiles : (away + 1) * tiles], Z * away) for away in range(1, ring)
    ]
    return in_vmem(
        functools.partial(last_kernel, ring),
        parts + [energy, vector, answer, residual],
        [(1, tiles, TILE)] * 2,
    )


def from_behind(shard, axis, by):
    devices = lax.axis_size(axis)
    return lax.ppermute(shard, axis, [(i, (i + by) % devices) for i in range(devices)])


def many_groups(rhs, damp_cam, precond, problem, tile_ids, counts):
    group_tiles = lax.axis_size("pts") * rhs.shape[0]
    halfway = group_tiles // 2
    window = 2 * group_tiles
    tables = tables_of(tile_ids, counts, window)

    def product(vector):
        panel = lax.all_gather(widen(vector), "pts", axis=0, tiled=True)
        lower = from_behind(panel[halfway:], "cam", 1)
        upper = from_behind(panel[:halfway], "cam", -1)
        whole_window = jnp.concatenate([lower, panel, upper], axis=0)
        partial = call_product(
            functools.partial(plain_kernel, len(problem)), problem, tables + [whole_window], [(window, WIDTH)]
        )[0]
        from_above = from_behind(partial[:halfway], "cam", -1)
        from_below = from_behind(partial[halfway + group_tiles :], "cam", 1)
        summed = partial[halfway : halfway + group_tiles] + jnp.concatenate(
            [from_below, from_above], axis=0
        )
        return lax.psum_scatter(summed, "pts", scatter_dimension=0, tiled=True)[:, :TILE] + damp_cam * vector

    def inner(one, two):
        return lax.psum(jnp.sum(one * two), AXES)

    answer, residual = jnp.zeros(rhs.shape, jnp.float32), rhs
    scaled = precond * residual
    direction = scaled
    energy = inner(residual, scaled)
    for iteration in range(ITERS):
        mapped = product(direction)
        step_size = energy / inner(direction, mapped)
        answer = answer + step_size * direction
        residual = residual - step_size * mapped
        scaled = precond * residual
        energy_next = inner(residual, scaled)
        direction = scaled + energy_next / energy * direction
        energy = energy_next
    return answer[None], residual[None]


def on_device(rhs, damp_cam, precond, cam_jac, pt_jac, damp_pt, cam_index, tile_ids, counts):
    arrays = (
        counts[0],
        jnp.transpose(cam_jac[0], (0, 2, 1, 3)),
        jnp.transpose(pt_jac[0], (0, 2, 1, 3)),
        cam_index[0],
        jnp.transpose(damp_pt[0], (1, 0, 2)),
    )
    chunks = math.gcd(cam_jac.shape[1], CHUNKS)
    tiles = cam_jac.shape[1] // chunks
    problem = [call_setup(chunk * tiles, tiles, *arrays) for chunk in range(chunks)]
    groups, shards = lax.axis_size("cam"), lax.axis_size("pts")
    plan = two_groups if groups == 2 and shards in (4, 8, 16, 32) else many_groups
    return tuple(plan(rhs[0], damp_cam[0], precond[0], problem, tile_ids[0], counts[0]))


def solution(mesh):
    return jax.shard_map(
        on_device,
        mesh=mesh,
        in_specs=(
            P("cam", "pts", None),
            P("cam", "pts", None),
            P("cam", "pts", None),
            P("cam", "pts", None, None, None),
            P("cam", "pts", None, None, None),
            P("cam", "pts", None, None),
            P("cam", "pts", None, None),
            P("cam", "pts", None),
            P("cam", "pts"),
        ),
        out_specs=(P("cam", "pts", None), P("cam", "pts", None)),
        check_vma=False,
    )
```

```python
import functools
import math

import jax
import jax.numpy as jnp
from jax import lax
from jax.experimental import pallas as pl
from jax.experimental.pallas import tpu as pltpu
from jax.sharding import PartitionSpec as P

ITERS = 3
CPAR = 9
CAMERAS = 64
SLOTS = 8
POINTS = 128
TILE = CPAR * CAMERAS
PAIRS = 5
WIDTH = PAIRS * 128
CHUNKS = 2
PARTS = 3
AXES = ("pts", "cam")


def split_two(value):
    high = value.astype(jnp.bfloat16)
    low = (value - high.astype(jnp.float32)).astype(jnp.bfloat16)
    return high, low


def all_slots(value):
    for by in (4, 2, 1):
        value = value + pltpu.roll(value, by, 0)
    return value


def stack_sums(values):
    row = lax.broadcasted_iota(jnp.int32, values[0].shape, 0)
    upper = row < 4
    values = [
        jnp.where(upper, one, two) + pltpu.roll(jnp.where(upper, two, one), 4, 0)
        for one, two in zip(values[:4], values[4:])
    ]
    for by in (2, 1):
        first = (row & by) == 0
        half = len(values) // 2
        values = [
            jnp.where(first, one + pltpu.roll(one, 8 - by, 0), two + pltpu.roll(two, by, 0))
            for one, two in zip(values[:half], values[half:])
        ]
    return values[0]


def invert(gram):
    a, b, c, d, e, f = gram
    aa = d * f - e * e
    bb = c * e - b * f
    cc = b * e - c * d
    dd = a * f - c * c
    ee = b * c - a * e
    ff = a * d - b * b
    scale = 1.0 / (a * aa + b * bb + c * cc)
    return [entry * scale for entry in (aa, bb, cc, dd, ee, ff)]


def setup_kernel(
    skip, group, counts, cam, point, index, damp,
    cam_out, point_out, index_out, inverse_out, selector_out, damping, arrived,
):
    tiles = cam_out.shape[0]
    turns = tiles // group

    def copy(array, out, turn, kind):
        here = pl.ds(turn * group, group)
        there = pl.ds(skip + turn * group, group)
        return pltpu.make_async_copy(array.at[there], out.at[here], arrived.at[kind, turn])

    damping_copy = pltpu.make_async_copy(damp.at[:, pl.ds(skip, tiles)], damping, arrived.at[3, 0])
    damping_copy.start()
    for kind, (array, out) in enumerate(((point, point_out), (index, index_out), (cam, cam_out))):
        for turn in range(turns):
            copy(array, out, turn, kind).start()
    slot = lax.broadcasted_iota(jnp.int32, (SLOTS, POINTS), 0)
    camera = lax.broadcasted_iota(jnp.int32, (CAMERAS, POINTS), 0).astype(jnp.bfloat16)
    one = jnp.ones((CAMERAS, POINTS), jnp.bfloat16)
    zero = jnp.zeros((CAMERAS, POINTS), jnp.bfloat16)
    damping_copy.wait()
    for turn in range(turns):
        copy(point, point_out, turn, 0).wait()
        copy(index, index_out, turn, 1).wait()
        here = range(turn * group, (turn + 1) * group)
        grams = []
        for i in here:
            live = (slot < counts[skip + i]).astype(jnp.float32)
            rows = [point_out[i, r] * live for r in range(6)]
            entries = [(0, 0), (0, 1), (0, 2), (1, 1), (1, 2), (2, 2)]
            grams.append([rows[a] * rows[b] + rows[3 + a] * rows[3 + b] for a, b in entries])
        gram = [stack_sums([one[a] for one in grams]) for a in range(6)]
        for a, entry in enumerate((0, 3, 5)):
            gram[entry] = gram[entry] + damping[a, turn * group : (turn + 1) * group, :]
        inverse = invert(gram)
        for turned, i in enumerate(here):
            for a in range(6):
                inverse_out[i, a] = jnp.broadcast_to(inverse[a][turned : turned + 1, :], slot.shape)
            wide = index_out[i].astype(jnp.float32)
            for k in range(SLOTS):
                row = wide[k : k + 1, :].astype(jnp.bfloat16)
                down, right = k // 2 * CAMERAS, k % 2 * POINTS
                selector_out[i, down : down + CAMERAS, right : right + POINTS] = jnp.where(
                    camera == row, one, zero
                )
    for turn in range(turns):
        copy(cam, cam_out, turn, 2).wait()


def tile_product(cam, point, index, inverse, selector, picked_from, row, put_to):
    slot = lax.broadcasted_iota(jnp.int32, (SLOTS, POINTS), 0)
    lane = lax.broadcasted_iota(jnp.int32, (SLOTS, POINTS), 1)
    other = index + CAMERAS
    pairs = [picked_from[pl.ds(row, SLOTS), p * 128 : (p + 1) * 128] for p in range(PAIRS)]
    picked = [
        jnp.take_along_axis(
            pairs[j // 2], other if j % 2 else index, axis=1, mode="promise_in_bounds"
        )
        for j in range(CPAR)
    ]
    rows = [point(r) for r in range(6)]
    q = []
    for r in range(2):
        total = cam(9 * r) * picked[0]
        for j in range(1, CPAR):
            total = total + cam(9 * r + j) * picked[j]
        q.append(total)
    y = [all_slots(rows[a] * q[0] + rows[3 + a] * q[1]) for a in range(3)]
    i0, i1, i2, i3, i4, i5 = [inverse(a) for a in range(6)]
    z = [
        i0 * y[0] + i1 * y[1] + i2 * y[2],
        i1 * y[0] + i3 * y[1] + i4 * y[2],
        i2 * y[0] + i4 * y[1] + i5 * y[2],
    ]
    e = [
        q[r] - (rows[3 * r] * z[0] + rows[3 * r + 1] * z[1] + rows[3 * r + 2] * z[2])
        for r in range(2)
    ]
    slot_twice = lax.broadcasted_iota(jnp.int32, (2 * SLOTS, POINTS), 0) & 1
    odd = slot_twice.astype(jnp.bfloat16)
    even = (1 - slot_twice).astype(jnp.bfloat16)
    returned = [cam(j) * e[0] + cam(9 + j) * e[1] for j in range(CPAR)]
    left = []
    for p in range(PAIRS - 1):
        left += split_two(jnp.concatenate(returned[2 * p : 2 * p + 2], axis=0))
    high = returned[-1].astype(jnp.bfloat16).astype(jnp.float32)
    left.append(jnp.concatenate([high, returned[-1] - high], axis=0).astype(jnp.bfloat16))
    left = jnp.concatenate(
        [jnp.concatenate([rows * even, rows * odd], axis=1) for rows in left], axis=0
    )
    spread = lax.dot_general(
        left, selector, (((1,), (1,)), ((), ())), preferred_element_type=jnp.float32
    )
    side = (slot >> 1) & 1
    first_side = side == 0
    keep = (lane >> 6) == side
    sums = []
    for j in range(CPAR):
        first = 32 * (j // 2) + 8 * (j % 2)
        second = first + (16 if j < CPAR - 1 else 8)
        both = spread[first : first + 8] + spread[second : second + 8]
        sums.append(jnp.where(slot < 4, both[:, :128], both[:, 128:]))
    sums.append(jnp.zeros_like(sums[0]))
    for p in range(PAIRS):
        one, two = sums[2 * p], sums[2 * p + 1]
        stay = jnp.where(first_side, one, two)
        move = pltpu.roll(jnp.where(first_side, two, one), CAMERAS, 1)
        put_to[pl.ds(row, SLOTS), p * 128 : (p + 1) * 128] = jnp.where(keep, stay, move)
    return q[0] * e[0] + q[1] * e[1]


def product_steps(problem, pick, put, vector, out, picked_from, put_to):
    parts = len(picked_from)
    share = sum(chunk[0].shape[0] for chunk in problem) // parts
    rows = share * SLOTS
    high, low = split_two(vector[...])

    def pick_part(part, p):
        table = pick[part * rows : (part + 1) * rows, :]
        here = slice(p * 128, (p + 1) * 128)
        both = jnp.concatenate([high[:, here], low[:, here]], axis=1)
        found = jnp.dot(table, both, preferred_element_type=jnp.float32)
        picked_from[part][:, here] = found[:, :128] + found[:, 128:]

    def put_part(part, p):
        table = put[:, part * rows : (part + 1) * rows]
        here = slice(p * 128, (p + 1) * 128)
        both = jnp.concatenate(split_two(put_to[part][:, here]), axis=1)
        found = jnp.dot(table, both, preferred_element_type=jnp.float32)
        found = found[:, :128] + found[:, 128:]
        out[:, here] = found if part == 0 else out[:, here] + found

    total = jnp.zeros((SLOTS, POINTS), jnp.float32)
    tiles = [(chunk, i) for chunk in problem for i in range(chunk[0].shape[0])]
    for p in range(PAIRS):
        pick_part(0, p)
    for part in range(parts):
        jobs = [functools.partial(pick_part, part + 1, p) for p in range(PAIRS)] if part + 1 < parts else []
        jobs += [functools.partial(put_part, part - 1, p) for p in range(PAIRS)] if part else []
        for turn, ((cam, point, index, inverse, selector), i) in enumerate(tiles[part * share : (part + 1) * share]):
            due = len(jobs) * turn // share
            if due > len(jobs) * (turn - 1) // share and turn:
                jobs[due - 1]()
            total = total + tile_product(
                lambda r: cam[i, r],
                lambda r: point[i, r],
                index[i],
                lambda a: inverse[i, a],
                selector[i],
                picked_from[part],
                turn * SLOTS,
                put_to[part],
            )
        if jobs:
            jobs[-1]()
    for p in range(PAIRS):
        put_part(parts - 1, p)
    return total


def total_of(value):
    return jnp.sum(value, keepdims=True).reshape(1, 1)


def in_spare(rows, value):
    lane = lax.broadcasted_iota(jnp.int32, (rows, 128), 1)
    return jnp.where(lane >= TILE - (WIDTH - 128), value, 0.0)


def spare_of(ref):
    return ref[0:1, TILE : TILE + 1]


def offer(residual, scaling, scaled):
    value = scaling[...] * residual[...]
    scaled[...] = value
    part = total_of(value * residual[...])
    scaled[:, WIDTH - 128 :] += in_spare(scaled.shape[0], part)


def start_kernel(*refs):
    pieces, (residual, scaling, scaled) = refs[:-4], refs[-3:]
    rows = pieces[0].shape[1]
    for away, piece in enumerate(pieces):
        residual[away * rows : (away + 1) * rows, :] = piece[0]
        scaling[away * rows : (away + 1) * rows, :] = piece[1]
    offer(residual, scaling, scaled)


def turn_kernel(ring, *refs):
    pieces, refs = refs[:ring], refs[ring:]
    energy, vector, old_answer, old_residual, scaling, answer, residual, scaled = refs
    rows = answer.shape[0]
    step_size = energy[0:1, 0:1] / sum([spare_of(piece) for piece in pieces])
    for b in range(ring):
        here = slice(b * rows, (b + 1) * rows)
        mapped = pieces[0][here, :]
        for a in range(1, ring):
            mapped = mapped + pieces[a][(a ^ b) * rows : ((a ^ b) + 1) * rows, :]
        residual[here, :] = old_residual[here, :] - step_size * mapped
    answer[...] = old_answer[...] + step_size * vector[:rows, :]
    offer(residual, scaling, scaled)


def last_kernel(ring, *refs):
    pieces, (energy, vector, old_answer, old_residual, answer, residual) = refs[:ring], refs[ring:]
    rows = old_answer.shape[0]
    mapped = sum([piece[...] for piece in pieces[1:]], pieces[0][...])
    step_size = energy[0:1, 0:1] / mapped[0:1, TILE : TILE + 1]
    answer[0] = (old_answer[...] + step_size * vector[:rows, :])[:, :TILE]
    residual[0] = (old_residual[:rows, :] - step_size * mapped)[:, :TILE]


def step_kernel(chunks, ranks, first, *refs):
    problem = [refs[5 * c : 5 * c + 5] for c in range(chunks)]
    (pick, put, damp), refs = refs[5 * chunks : 5 * chunks + 3], refs[5 * chunks + 3 :]
    pieces, refs = refs[:ranks], refs[ranks:]
    if not first:
        (old_vector, old_energy), refs = refs[:2], refs[2:]
    (out, vector, energy), scratch = refs[:3], refs[3:]
    picked_from, put_to = scratch[: len(scratch) // 2], scratch[len(scratch) // 2 :]
    power = sum([spare_of(piece) for piece in pieces])
    energy[...] = jnp.broadcast_to(power, energy.shape)
    many = pieces[0].shape[0]
    for r in range(ranks):
        part = slice(r * many, (r + 1) * many)
        if first:
            vector[part, :] = pieces[r][...]
        else:
            vector[part, :] = pieces[r][...] + (power / old_energy[0:1, 0:1]) * old_vector[part, :]
    dot = product_steps(problem, pick, put, vector, out, picked_from, put_to)
    rows = damp.shape[0]
    damped = damp[...] * vector[:rows, :]
    out[:rows, :] += damped
    out[:, WIDTH - 128 :] += in_spare(out.shape[0], total_of(dot) + total_of(damped * vector[:rows, :]))


def plain_kernel(chunks, *refs):
    problem = [refs[5 * c : 5 * c + 5] for c in range(chunks)]
    (pick, put, vector, out), scratch = refs[5 * chunks : 5 * chunks + 4], refs[5 * chunks + 4 :]
    picked_from, put_to = scratch[: len(scratch) // 2], scratch[len(scratch) // 2 :]
    product_steps(problem, pick, put, vector, out, picked_from, put_to)


def in_vmem(kernel, operands, outs, scratch=()):
    spec = pl.BlockSpec(memory_space=pltpu.VMEM)
    return pl.pallas_call(
        kernel,
        out_shape=[jax.ShapeDtypeStruct(shape, jnp.float32) for shape in outs],
        in_specs=[spec] * len(operands),
        out_specs=[spec] * len(outs),
        scratch_shapes=list(scratch),
        compiler_params=pltpu.CompilerParams(vmem_limit_bytes=20 * 2**20),
    )(*operands)


def call_setup(skip, tiles, counts, cam, point, index, damp):
    group = SLOTS
    shapes = [(tiles,) + array.shape[1:] for array in (cam, point, index)]
    shapes += [(tiles, 6, SLOTS, POINTS), (tiles, SLOTS // 2 * CAMERAS, 2 * POINTS)]
    kinds = [jnp.float32, jnp.float32, jnp.int32, jnp.float32, jnp.bfloat16]
    return pl.pallas_call(
        functools.partial(setup_kernel, skip, group),
        out_shape=[pltpu.VMEM(shape, kind) for shape, kind in zip(shapes, kinds)],
        in_specs=[pl.BlockSpec(memory_space=pltpu.SMEM)] + [pl.BlockSpec(memory_space=pltpu.HBM)] * 4,
        out_specs=[pl.BlockSpec(memory_space=pltpu.VMEM)] * 5,
        scratch_shapes=[
            pltpu.VMEM((3, tiles, POINTS), jnp.float32),
            pltpu.SemaphoreType.DMA((4, tiles // group)),
        ],
        compiler_params=pltpu.CompilerParams(vmem_limit_bytes=4 * 2**20),
        cost_estimate=pl.CostEstimate(flops=3 * 10**7, bytes_accessed=10**7, transcendentals=0),
    )(counts, *[pltpu.with_memory_space_constraint(x, pltpu.HBM) for x in (cam, point, index, damp)])


def call_product(kernel, problem, others, outs):
    tiles = sum(chunk[0].shape[0] for chunk in problem)
    parts = math.gcd(tiles, PARTS)
    scratch = pltpu.VMEM((tiles // parts * SLOTS, WIDTH), jnp.float32)
    held = [pltpu.with_memory_space_constraint(array, pltpu.VMEM) for chunk in problem for array in chunk]
    return in_vmem(kernel, held + others, outs, [scratch] * (2 * parts))


def tables_of(rows, counts, window):
    live = lax.iota(jnp.int32, SLOTS)[None, :] < counts[:, None]
    listed = jnp.where(live, rows, -1).reshape(-1)
    places = lax.iota(jnp.int32, window)
    pick = (listed[:, None] == places[None, :]).astype(jnp.bfloat16)
    put = (places[:, None] == listed[None, :]).astype(jnp.bfloat16)
    return [pick, put]


def widen(array):
    return jnp.pad(array, [(0, 0)] * (array.ndim - 1) + [(0, WIDTH - TILE)])


def exchange(array, mask):
    devices = lax.axis_size("pts") * lax.axis_size("cam")
    return lax.ppermute(array, AXES, [(i, i ^ mask) for i in range(devices)])


def two_groups(rhs, damp_cam, precond, problem, tile_ids, counts):
    CAM, CORE, Y, Z = 1, 2, 4, 8
    shards = lax.axis_size("pts")
    tiles = rhs.shape[0]
    ring = shards // 4
    group, shard = lax.axis_index("cam"), lax.axis_index("pts")
    group_tiles = shards * tiles
    window = 2 * group_tiles
    where = (group * group_tiles + tile_ids - group_tiles // 2) % window
    owner_group, owner = where // group_tiles, where % group_tiles // tiles
    apart = owner ^ shard
    rank = (apart & 1) * 4 + (owner_group ^ group) * 2 + ((apart >> 1) & 1)
    tables = tables_of((rank * ring + (apart >> 2)) * tiles + where % tiles, counts, window)
    steady = tables + [widen(damp_cam)]

    def gather(own, ahead=None):
        near = [own, exchange(own, Y), exchange(own, CAM), exchange(own, CAM | Y)]
        if ahead is not None:
            near = list(lax.optimization_barrier((*near, ahead)))[:4]
        return near + [exchange(piece, CORE) for piece in near]

    def reduce(partial):
        half = window // 2
        mine = partial[:half] + exchange(partial[half:], CORE)
        part = half // 4
        return (
            mine[:part]
            + exchange(mine[part : 2 * part], Y)
            + exchange(mine[2 * part : 3 * part], CAM)
            + exchange(mine[3 * part :], CAM | Y)
        )

    full, line, small, own = (window, WIDTH), (ring * tiles, WIDTH), (8, 128), (tiles, WIDTH)
    both = widen(jnp.stack([rhs, precond]))
    both = [both] + [exchange(both, Z * away) for away in range(1, ring)]
    residual, scaling, scaled = in_vmem(start_kernel, both + [problem[0][2]], [line, line, line])
    answer = jnp.zeros(own, jnp.float32)
    known = []
    for iteration in range(ITERS):
        partial, vector, energy = call_product(
            functools.partial(step_kernel, len(problem), 8, iteration == 0),
            problem, steady + gather(scaled, problem[-1][2] if iteration == 0 else None) + known, [full, full, small],
        )
        known = [vector, energy]
        mine = reduce(partial)
        if iteration + 1 < ITERS:
            parts = [mine] + [exchange(mine, Z * away) for away in range(1, ring)]
            answer, residual, scaled = in_vmem(
                functools.partial(turn_kernel, ring),
                parts + [energy, vector, answer, residual, scaling],
                [own, line, line],
            )
    parts = [mine[:tiles]] + [
        exchange(mine[away * tiles : (away + 1) * tiles], Z * away) for away in range(1, ring)
    ]
    return in_vmem(
        functools.partial(last_kernel, ring),
        parts + [energy, vector, answer, residual],
        [(1, tiles, TILE)] * 2,
    )


def from_behind(shard, axis, by):
    devices = lax.axis_size(axis)
    return lax.ppermute(shard, axis, [(i, (i + by) % devices) for i in range(devices)])


def many_groups(rhs, damp_cam, precond, problem, tile_ids, counts):
    group_tiles = lax.axis_size("pts") * rhs.shape[0]
    halfway = group_tiles // 2
    window = 2 * group_tiles
    tables = tables_of(tile_ids, counts, window)

    def product(vector):
        panel = lax.all_gather(widen(vector), "pts", axis=0, tiled=True)
        lower = from_behind(panel[halfway:], "cam", 1)
        upper = from_behind(panel[:halfway], "cam", -1)
        whole_window = jnp.concatenate([lower, panel, upper], axis=0)
        partial = call_product(
            functools.partial(plain_kernel, len(problem)), problem, tables + [whole_window], [(window, WIDTH)]
        )[0]
        from_above = from_behind(partial[:halfway], "cam", -1)
        from_below = from_behind(partial[halfway + group_tiles :], "cam", 1)
        summed = partial[halfway : halfway + group_tiles] + jnp.concatenate(
            [from_below, from_above], axis=0
        )
        return lax.psum_scatter(summed, "pts", scatter_dimension=0, tiled=True)[:, :TILE] + damp_cam * vector

    def inner(one, two):
        return lax.psum(jnp.sum(one * two), AXES)

    answer, residual = jnp.zeros(rhs.shape, jnp.float32), rhs
    scaled = precond * residual
    direction = scaled
    energy = inner(residual, scaled)
    for iteration in range(ITERS):
        mapped = product(direction)
        step_size = energy / inner(direction, mapped)
        answer = answer + step_size * direction
        residual = residual - step_size * mapped
        scaled = precond * residual
        energy_next = inner(residual, scaled)
        direction = scaled + energy_next / energy * direction
        energy = energy_next
    return answer[None], residual[None]


def on_device(rhs, damp_cam, precond, cam_jac, pt_jac, damp_pt, cam_index, tile_ids, counts):
    arrays = (
        counts[0],
        jnp.transpose(cam_jac[0], (0, 2, 1, 3)),
        jnp.transpose(pt_jac[0], (0, 2, 1, 3)),
        cam_index[0],
        jnp.transpose(damp_pt[0], (1, 0, 2)),
    )
    chunks = math.gcd(cam_jac.shape[1], CHUNKS)
    tiles = cam_jac.shape[1] // chunks
    problem = [call_setup(chunk * tiles, tiles, *arrays) for chunk in range(chunks)]
    groups, shards = lax.axis_size("cam"), lax.axis_size("pts")
    plan = two_groups if groups == 2 and shards in (4, 8, 16, 32) else many_groups
    return tuple(plan(rhs[0], damp_cam[0], precond[0], problem, tile_ids[0], counts[0]))


def solution(mesh):
    return jax.shard_map(
        on_device,
        mesh=mesh,
        in_specs=(
            P("cam", "pts", None),
            P("cam", "pts", None),
            P("cam", "pts", None),
            P("cam", "pts", None, None, None),
            P("cam", "pts", None, None, None),
            P("cam", "pts", None, None),
            P("cam", "pts", None, None),
            P("cam", "pts", None),
            P("cam", "pts"),
        ),
        out_specs=(P("cam", "pts", None), P("cam", "pts", None)),
        check_vma=False,
    )
```

```python
import functools
import math

import jax
import jax.numpy as jnp
from jax import lax
from jax.experimental import pallas as pl
from jax.experimental.pallas import tpu as pltpu
from jax.sharding import PartitionSpec as P

ITERS = 3
CPAR = 9
CAMERAS = 64
SLOTS = 8
POINTS = 128
TILE = CPAR * CAMERAS
PAIRS = 5
WIDTH = PAIRS * 128
PARTS = 3
AXES = ("pts", "cam")


def split_two(value):
    high = value.astype(jnp.bfloat16)
    low = (value - high.astype(jnp.float32)).astype(jnp.bfloat16)
    return high, low


def all_slots(value):
    for by in (4, 2, 1):
        value = value + pltpu.roll(value, by, 0)
    return value


def stack_sums(values):
    row = lax.broadcasted_iota(jnp.int32, values[0].shape, 0)
    upper = row < 4
    values = [
        jnp.where(upper, one, two) + pltpu.roll(jnp.where(upper, two, one), 4, 0)
        for one, two in zip(values[:4], values[4:])
    ]
    for by in (2, 1):
        first = (row & by) == 0
        half = len(values) // 2
        values = [
            jnp.where(first, one + pltpu.roll(one, 8 - by, 0), two + pltpu.roll(two, by, 0))
            for one, two in zip(values[:half], values[half:])
        ]
    return values[0]


def invert(gram):
    a, b, c, d, e, f = gram
    aa = d * f - e * e
    bb = c * e - b * f
    cc = b * e - c * d
    dd = a * f - c * c
    ee = b * c - a * e
    ff = a * d - b * b
    scale = 1.0 / (a * aa + b * bb + c * cc)
    return [entry * scale for entry in (aa, bb, cc, dd, ee, ff)]


def setup_kernel(
    skip, group, counts, cam, point, index, damp,
    cam_out, point_out, index_out, inverse_out, selector_out, damping, arrived,
):
    tiles = cam_out.shape[0]
    turns = tiles // group

    def copy(array, out, turn, kind):
        here = pl.ds(turn * group, group)
        there = pl.ds(skip + turn * group, group)
        return pltpu.make_async_copy(array.at[there], out.at[here], arrived.at[kind, turn])

    damping_copy = pltpu.make_async_copy(damp.at[:, pl.ds(skip, tiles)], damping, arrived.at[3, 0])
    damping_copy.start()
    for kind, (array, out) in enumerate(((point, point_out), (index, index_out), (cam, cam_out))):
        for turn in range(turns):
            copy(array, out, turn, kind).start()
    slot = lax.broadcasted_iota(jnp.int32, (SLOTS, POINTS), 0)
    camera = lax.broadcasted_iota(jnp.int32, (CAMERAS, POINTS), 0).astype(jnp.bfloat16)
    one = jnp.ones((CAMERAS, POINTS), jnp.bfloat16)
    zero = jnp.zeros((CAMERAS, POINTS), jnp.bfloat16)
    damping_copy.wait()
    for turn in range(turns):
        copy(point, point_out, turn, 0).wait()
        copy(index, index_out, turn, 1).wait()
        here = range(turn * group, (turn + 1) * group)
        grams = []
        for i in here:
            live = (slot < counts[skip + i]).astype(jnp.float32)
            rows = [point_out[i, r] * live for r in range(6)]
            entries = [(0, 0), (0, 1), (0, 2), (1, 1), (1, 2), (2, 2)]
            grams.append([rows[a] * rows[b] + rows[3 + a] * rows[3 + b] for a, b in entries])
        gram = [stack_sums([one[a] for one in grams]) for a in range(6)]
        for a, entry in enumerate((0, 3, 5)):
            gram[entry] = gram[entry] + damping[a, turn * group : (turn + 1) * group, :]
        inverse = invert(gram)
        for turned, i in enumerate(here):
            for a in range(6):
                inverse_out[i, a] = jnp.broadcast_to(inverse[a][turned : turned + 1, :], slot.shape)
            wide = index_out[i].astype(jnp.float32)
            for k in range(SLOTS):
                row = wide[k : k + 1, :].astype(jnp.bfloat16)
                down, right = k // 2 * CAMERAS, k % 2 * POINTS
                selector_out[i, down : down + CAMERAS, right : right + POINTS] = jnp.where(
                    camera == row, one, zero
                )
    for turn in range(turns):
        copy(cam, cam_out, turn, 2).wait()


def tile_product(cam, point, index, inverse, selector, picked_from, row, put_to):
    slot = lax.broadcasted_iota(jnp.int32, (SLOTS, POINTS), 0)
    lane = lax.broadcasted_iota(jnp.int32, (SLOTS, POINTS), 1)
    other = index + CAMERAS
    pairs = [picked_from[pl.ds(row, SLOTS), p * 128 : (p + 1) * 128] for p in range(PAIRS)]
    picked = [
        jnp.take_along_axis(
            pairs[j // 2], other if j % 2 else index, axis=1, mode="promise_in_bounds"
        )
        for j in range(CPAR)
    ]
    rows = [point(r) for r in range(6)]
    q = []
    for r in range(2):
        total = cam(9 * r) * picked[0]
        for j in range(1, CPAR):
            total = total + cam(9 * r + j) * picked[j]
        q.append(total)
    y = [all_slots(rows[a] * q[0] + rows[3 + a] * q[1]) for a in range(3)]
    i0, i1, i2, i3, i4, i5 = [inverse(a) for a in range(6)]
    z = [
        i0 * y[0] + i1 * y[1] + i2 * y[2],
        i1 * y[0] + i3 * y[1] + i4 * y[2],
        i2 * y[0] + i4 * y[1] + i5 * y[2],
    ]
    e = [
        q[r] - (rows[3 * r] * z[0] + rows[3 * r + 1] * z[1] + rows[3 * r + 2] * z[2])
        for r in range(2)
    ]
    slot_twice = lax.broadcasted_iota(jnp.int32, (2 * SLOTS, POINTS), 0) & 1
    odd = slot_twice.astype(jnp.bfloat16)
    even = (1 - slot_twice).astype(jnp.bfloat16)
    returned = [cam(j) * e[0] + cam(9 + j) * e[1] for j in range(CPAR)]
    left = []
    for p in range(PAIRS - 1):
        left += split_two(jnp.concatenate(returned[2 * p : 2 * p + 2], axis=0))
    high = returned[-1].astype(jnp.bfloat16).astype(jnp.float32)
    left.append(jnp.concatenate([high, returned[-1] - high], axis=0).astype(jnp.bfloat16))
    left = jnp.concatenate(
        [jnp.concatenate([rows * even, rows * odd], axis=1) for rows in left], axis=0
    )
    spread = lax.dot_general(
        left, selector, (((1,), (1,)), ((), ())), preferred_element_type=jnp.float32
    )
    side = (slot >> 1) & 1
    first_side = side == 0
    keep = (lane >> 6) == side
    sums = []
    for j in range(CPAR):
        first = 32 * (j // 2) + 8 * (j % 2)
        second = first + (16 if j < CPAR - 1 else 8)
        both = spread[first : first + 8] + spread[second : second + 8]
        sums.append(jnp.where(slot < 4, both[:, :128], both[:, 128:]))
    sums.append(jnp.zeros_like(sums[0]))
    for p in range(PAIRS):
        one, two = sums[2 * p], sums[2 * p + 1]
        stay = jnp.where(first_side, one, two)
        move = pltpu.roll(jnp.where(first_side, two, one), CAMERAS, 1)
        put_to[pl.ds(row, SLOTS), p * 128 : (p + 1) * 128] = jnp.where(keep, stay, move)
    return q[0] * e[0] + q[1] * e[1]


def product_steps(problem, pick, put, vector, out, picked_from, put_to):
    parts = len(picked_from)
    share = sum(chunk[0].shape[0] for chunk in problem) // parts
    rows = share * SLOTS
    high, low = split_two(vector[...])

    def pick_part(part, p):
        table = pick[part * rows : (part + 1) * rows, :]
        here = slice(p * 128, (p + 1) * 128)
        both = jnp.concatenate([high[:, here], low[:, here]], axis=1)
        found = jnp.dot(table, both, preferred_element_type=jnp.float32)
        picked_from[part][:, here] = found[:, :128] + found[:, 128:]

    def put_part(part, p):
        table = put[:, part * rows : (part + 1) * rows]
        here = slice(p * 128, (p + 1) * 128)
        both = jnp.concatenate(split_two(put_to[part][:, here]), axis=1)
        found = jnp.dot(table, both, preferred_element_type=jnp.float32)
        found = found[:, :128] + found[:, 128:]
        out[:, here] = found if part == 0 else out[:, here] + found

    total = jnp.zeros((SLOTS, POINTS), jnp.float32)
    tiles = [(chunk, i) for chunk in problem for i in range(chunk[0].shape[0])]
    for p in range(PAIRS):
        pick_part(0, p)
    for part in range(parts):
        jobs = [functools.partial(pick_part, part + 1, p) for p in range(PAIRS)] if part + 1 < parts else []
        jobs += [functools.partial(put_part, part - 1, p) for p in range(PAIRS)] if part else []
        for turn, ((cam, point, index, inverse, selector), i) in enumerate(tiles[part * share : (part + 1) * share]):
            due = len(jobs) * turn // share
            if due > len(jobs) * (turn - 1) // share and turn:
                jobs[due - 1]()
            total = total + tile_product(
                lambda r: cam[i, r],
                lambda r: point[i, r],
                index[i],
                lambda a: inverse[i, a],
                selector[i],
                picked_from[part],
                turn * SLOTS,
                put_to[part],
            )
        if jobs:
            jobs[-1]()
    for p in range(PAIRS):
        put_part(parts - 1, p)
    return total


def total_of(value):
    return jnp.sum(value, keepdims=True).reshape(1, 1)


def in_spare(rows, value):
    lane = lax.broadcasted_iota(jnp.int32, (rows, 128), 1)
    return jnp.where(lane >= TILE - (WIDTH - 128), value, 0.0)


def spare_of(ref):
    return ref[0:1, TILE : TILE + 1]


def offer(residual, scaling, scaled):
    value = scaling[...] * residual[...]
    scaled[...] = value
    part = total_of(value * residual[...])
    scaled[:, WIDTH - 128 :] += in_spare(scaled.shape[0], part)


def start_kernel(*refs):
    pieces, (residual, scaling, scaled) = refs[:-4], refs[-3:]
    rows = pieces[0].shape[1]
    for away, piece in enumerate(pieces):
        residual[away * rows : (away + 1) * rows, :] = piece[0]
        scaling[away * rows : (away + 1) * rows, :] = piece[1]
    offer(residual, scaling, scaled)


def turn_kernel(ring, *refs):
    pieces, refs = refs[:ring], refs[ring:]
    energy, vector, old_answer, old_residual, scaling, answer, residual, scaled = refs
    rows = answer.shape[0]
    step_size = energy[0:1, 0:1] / sum([spare_of(piece) for piece in pieces])
    for b in range(ring):
        here = slice(b * rows, (b + 1) * rows)
        mapped = pieces[0][here, :]
        for a in range(1, ring):
            mapped = mapped + pieces[a][(a ^ b) * rows : ((a ^ b) + 1) * rows, :]
        residual[here, :] = old_residual[here, :] - step_size * mapped
    answer[...] = old_answer[...] + step_size * vector[:rows, :]
    offer(residual, scaling, scaled)


def last_kernel(ring, *refs):
    pieces, (energy, vector, old_answer, old_residual, answer, residual) = refs[:ring], refs[ring:]
    rows = old_answer.shape[0]
    mapped = sum([piece[...] for piece in pieces[1:]], pieces[0][...])
    step_size = energy[0:1, 0:1] / mapped[0:1, TILE : TILE + 1]
    answer[0] = (old_answer[...] + step_size * vector[:rows, :])[:, :TILE]
    residual[0] = (old_residual[:rows, :] - step_size * mapped)[:, :TILE]


def step_kernel(chunks, ranks, first, *refs):
    problem = [refs[5 * c : 5 * c + 5] for c in range(chunks)]
    (pick, put, damp), refs = refs[5 * chunks : 5 * chunks + 3], refs[5 * chunks + 3 :]
    pieces, refs = refs[:ranks], refs[ranks:]
    if not first:
        (old_vector, old_energy), refs = refs[:2], refs[2:]
    (out, vector, energy), scratch = refs[:3], refs[3:]
    picked_from, put_to = scratch[: len(scratch) // 2], scratch[len(scratch) // 2 :]
    power = sum([spare_of(piece) for piece in pieces])
    energy[...] = jnp.broadcast_to(power, energy.shape)
    many = pieces[0].shape[0]
    for r in range(ranks):
        part = slice(r * many, (r + 1) * many)
        if first:
            vector[part, :] = pieces[r][...]
        else:
            vector[part, :] = pieces[r][...] + (power / old_energy[0:1, 0:1]) * old_vector[part, :]
    dot = product_steps(problem, pick, put, vector, out, picked_from, put_to)
    rows = damp.shape[0]
    damped = damp[...] * vector[:rows, :]
    out[:rows, :] += damped
    out[:, WIDTH - 128 :] += in_spare(out.shape[0], total_of(dot) + total_of(damped * vector[:rows, :]))


def plain_kernel(chunks, *refs):
    problem = [refs[5 * c : 5 * c + 5] for c in range(chunks)]
    (pick, put, vector, out), scratch = refs[5 * chunks : 5 * chunks + 4], refs[5 * chunks + 4 :]
    picked_from, put_to = scratch[: len(scratch) // 2], scratch[len(scratch) // 2 :]
    product_steps(problem, pick, put, vector, out, picked_from, put_to)


def in_vmem(kernel, operands, outs, scratch=()):
    spec = pl.BlockSpec(memory_space=pltpu.VMEM)
    return pl.pallas_call(
        kernel,
        out_shape=[jax.ShapeDtypeStruct(shape, jnp.float32) for shape in outs],
        in_specs=[spec] * len(operands),
        out_specs=[spec] * len(outs),
        scratch_shapes=list(scratch),
        compiler_params=pltpu.CompilerParams(vmem_limit_bytes=20 * 2**20),
    )(*operands)


def call_setup(skip, tiles, counts, cam, point, index, damp):
    group = SLOTS
    shapes = [(tiles,) + array.shape[1:] for array in (cam, point, index)]
    shapes += [(tiles, 6, SLOTS, POINTS), (tiles, SLOTS // 2 * CAMERAS, 2 * POINTS)]
    kinds = [jnp.float32, jnp.float32, jnp.int32, jnp.float32, jnp.bfloat16]
    return pl.pallas_call(
        functools.partial(setup_kernel, skip, group),
        out_shape=[pltpu.VMEM(shape, kind) for shape, kind in zip(shapes, kinds)],
        in_specs=[pl.BlockSpec(memory_space=pltpu.SMEM)] + [pl.BlockSpec(memory_space=pltpu.HBM)] * 4,
        out_specs=[pl.BlockSpec(memory_space=pltpu.VMEM)] * 5,
        scratch_shapes=[
            pltpu.VMEM((3, tiles, POINTS), jnp.float32),
            pltpu.SemaphoreType.DMA((4, tiles // group)),
        ],
        compiler_params=pltpu.CompilerParams(vmem_limit_bytes=4 * 2**20),
        cost_estimate=pl.CostEstimate(flops=3 * 10**7, bytes_accessed=10**7, transcendentals=0),
    )(*[pltpu.with_memory_space_constraint(x, pltpu.HBM) for x in (counts, cam, point, index, damp)])


def call_product(kernel, problem, others, outs):
    tiles = sum(chunk[0].shape[0] for chunk in problem)
    parts = math.gcd(tiles, PARTS)
    scratch = pltpu.VMEM((tiles // parts * SLOTS, WIDTH), jnp.float32)
    held = [pltpu.with_memory_space_constraint(array, pltpu.VMEM) for chunk in problem for array in chunk]
    return in_vmem(kernel, held + others, outs, [scratch] * (2 * parts))


def tables_of(rows, counts, window):
    live = lax.iota(jnp.int32, SLOTS)[None, :] < counts[:, None]
    listed = jnp.where(live, rows, -1).reshape(-1)
    places = lax.iota(jnp.int32, window)
    pick = (listed[:, None] == places[None, :]).astype(jnp.bfloat16)
    put = (places[:, None] == listed[None, :]).astype(jnp.bfloat16)
    return [pick, put]


def widen(array):
    return jnp.pad(array, [(0, 0)] * (array.ndim - 1) + [(0, WIDTH - TILE)])


def exchange(array, mask):
    devices = lax.axis_size("pts") * lax.axis_size("cam")
    return lax.ppermute(array, AXES, [(i, i ^ mask) for i in range(devices)])


def two_groups(rhs, damp_cam, precond, problem, tile_ids, counts):
    CAM, CORE, Y, Z = 1, 2, 4, 8
    shards = lax.axis_size("pts")
    tiles = rhs.shape[0]
    ring = shards // 4
    group, shard = lax.axis_index("cam"), lax.axis_index("pts")
    group_tiles = shards * tiles
    window = 2 * group_tiles
    where = (group * group_tiles + tile_ids - group_tiles // 2) % window
    owner_group, owner = where // group_tiles, where % group_tiles // tiles
    apart = owner ^ shard
    rank = (apart & 1) * 4 + (owner_group ^ group) * 2 + ((apart >> 1) & 1)
    tables = tables_of((rank * ring + (apart >> 2)) * tiles + where % tiles, counts, window)
    steady = tables + [widen(damp_cam)]

    def gather(own, ahead=None):
        near = [own, exchange(own, Y), exchange(own, CAM), exchange(own, CAM | Y)]
        if ahead is not None:
            near = list(lax.optimization_barrier((*near, ahead)))[:4]
        return near + [exchange(piece, CORE) for piece in near]

    def reduce(partial):
        half = window // 2
        mine = partial[:half] + exchange(partial[half:], CORE)
        part = half // 4
        return (
            mine[:part]
            + exchange(mine[part : 2 * part], Y)
            + exchange(mine[2 * part : 3 * part], CAM)
            + exchange(mine[3 * part :], CAM | Y)
        )

    full, line, small, own = (window, WIDTH), (ring * tiles, WIDTH), (8, 128), (tiles, WIDTH)
    both = widen(jnp.stack([rhs, precond]))
    both = [both] + [exchange(both, Z * away) for away in range(1, ring)]
    residual, scaling, scaled = in_vmem(start_kernel, both + [problem[0][2]], [line, line, line])
    answer = jnp.zeros(own, jnp.float32)
    known = []
    for iteration in range(ITERS):
        partial, vector, energy = call_product(
            functools.partial(step_kernel, len(problem), 8, iteration == 0),
            problem, steady + gather(scaled, problem[-1][2] if iteration == 0 else None) + known, [full, full, small],
        )
        known = [vector, energy]
        mine = reduce(partial)
        if iteration + 1 < ITERS:
            parts = [mine] + [exchange(mine, Z * away) for away in range(1, ring)]
            answer, residual, scaled = in_vmem(
                functools.partial(turn_kernel, ring),
                parts + [energy, vector, answer, residual, scaling],
                [own, line, line],
            )
    parts = [mine[:tiles]] + [
        exchange(mine[away * tiles : (away + 1) * tiles], Z * away) for away in range(1, ring)
    ]
    return in_vmem(
        functools.partial(last_kernel, ring),
        parts + [energy, vector, answer, residual],
        [(1, tiles, TILE)] * 2,
    )


def from_behind(shard, axis, by):
    devices = lax.axis_size(axis)
    return lax.ppermute(shard, axis, [(i, (i + by) % devices) for i in range(devices)])


def many_groups(rhs, damp_cam, precond, problem, tile_ids, counts):
    group_tiles = lax.axis_size("pts") * rhs.shape[0]
    halfway = group_tiles // 2
    window = 2 * group_tiles
    tables = tables_of(tile_ids, counts, window)

    def product(vector):
        panel = lax.all_gather(widen(vector), "pts", axis=0, tiled=True)
        lower = from_behind(panel[halfway:], "cam", 1)
        upper = from_behind(panel[:halfway], "cam", -1)
        whole_window = jnp.concatenate([lower, panel, upper], axis=0)
        partial = call_product(
            functools.partial(plain_kernel, len(problem)), problem, tables + [whole_window], [(window, WIDTH)]
        )[0]
        from_above = from_behind(partial[:halfway], "cam", -1)
        from_below = from_behind(partial[halfway + group_tiles :], "cam", 1)
        summed = partial[halfway : halfway + group_tiles] + jnp.concatenate(
            [from_below, from_above], axis=0
        )
        return lax.psum_scatter(summed, "pts", scatter_dimension=0, tiled=True)[:, :TILE] + damp_cam * vector

    def inner(one, two):
        return lax.psum(jnp.sum(one * two), AXES)

    answer, residual = jnp.zeros(rhs.shape, jnp.float32), rhs
    scaled = precond * residual
    direction = scaled
    energy = inner(residual, scaled)
    for iteration in range(ITERS):
        mapped = product(direction)
        step_size = energy / inner(direction, mapped)
        answer = answer + step_size * direction
        residual = residual - step_size * mapped
        scaled = precond * residual
        energy_next = inner(residual, scaled)
        direction = scaled + energy_next / energy * direction
        energy = energy_next
    return answer[None], residual[None]


def on_device(rhs, damp_cam, precond, cam_jac, pt_jac, damp_pt, cam_index, tile_ids, counts):
    arrays = (
        counts[0],
        jnp.transpose(cam_jac[0], (0, 2, 1, 3)),
        jnp.transpose(pt_jac[0], (0, 2, 1, 3)),
        cam_index[0],
        jnp.transpose(damp_pt[0], (1, 0, 2)),
    )
    tiles = cam_jac.shape[1]
    first = tiles * 5 // (12 * SLOTS) * SLOTS
    problem = [call_setup(0, first, *arrays), call_setup(first, tiles - first, *arrays)]
    groups, shards = lax.axis_size("cam"), lax.axis_size("pts")
    plan = two_groups if groups == 2 and shards in (4, 8, 16, 32) else many_groups
    return tuple(plan(rhs[0], damp_cam[0], precond[0], problem, tile_ids[0], counts[0]))


def solution(mesh):
    return jax.shard_map(
        on_device,
        mesh=mesh,
        in_specs=(
            P("cam", "pts", None),
            P("cam", "pts", None),
            P("cam", "pts", None),
            P("cam", "pts", None, None, None),
            P("cam", "pts", None, None, None),
            P("cam", "pts", None, None),
            P("cam", "pts", None, None),
            P("cam", "pts", None),
            P("cam", "pts"),
        ),
        out_specs=(P("cam", "pts", None), P("cam", "pts", None)),
        check_vma=False,
    )
```
